128 devices in a mesh: ctx: 32 (over z, y, core), exp: 4 (over x).
Axes of the slice: x: 4, y: 4, z: 4, core: 2. Of those that a mesh axis runs over, the one named last changes fastest.
Arguments:
- head_values: bfloat16 [8192, 8192], P('ctx', 'exp'), may hold values from -6 to 6
- gate_values: bfloat16 [8192, 8192], P('ctx', 'exp'), may hold values from -6 to 6
- write_keys: bfloat16 [8192, 128], P('ctx'), may hold values from -2 to 2
- read_keys: bfloat16 [8192, 128], P('ctx'), may hold values from -2 to 2
- step_size: float32 [8192, 64], P('ctx', 'exp'), may hold values from 0.012 to 0.21, as said below
- decay_rate: float32 [64], P('exp'), may hold values from 1.1765245e-05 to 0.67, as said below
- skip_weight: float32 [64], P('exp'), may hold values from 0.5 to 1.5
- prior_state: float32 [64, 128, 128], P('exp'), may hold values from -6 to 6
- norm_gain: float32 [8192], P('exp'), may hold values from 0.5 to 1.5
- out_weight: bfloat16 [8192, 8192], P('exp', 'ctx'), may hold values from -0.125 to 0.125
- residual: bfloat16 [8192, 8192], P('ctx', 'exp'), may hold values from -6 to 6
Outputs:
- layer_out: bfloat16 [8192, 8192], P('ctx', 'exp')
The draws below stay inside these ranges and needn't reach their ends.
Inputs may be any that keep to these rules, and one draw needn't show every extreme that they name: `step_size`: positive steps. `decay_rate`: positive rates.
All inputs are finite; a program needn't handle non-finite values.
Results may differ from the reference program's by a relative error of at most 0.0049.
Values may be sent and summed in bfloat16 or wider, within the bound.
No kernel may reach another device: no remote copies, remote signals or barrier semaphores. Data moves between devices by JAX's collectives and lax.ppermute only.
A program may use at most 192 MiB of HBM per device.

```python
import math
import jax
import jax.numpy as jnp
from jax import lax

D = 8192
HEADS = 64
HEAD_DIM = 128
STATE = 128
BLOCK = 256
INNER = 8192
TOKENS = 8192


def draw_step_size(key, part):
    key = jax.random.fold_in(key, 11)
    first_key, second_key = jax.random.split(key)
    rough = jnp.exp(jax.random.uniform(first_key, (TOKENS, HEADS), jnp.float32, -0.7, 0.7))
    blocks = jnp.exp(jax.random.uniform(second_key, (TOKENS // BLOCK, 1, HEADS), jnp.float32, -0.7, 0.7))
    shaped = rough.reshape(TOKENS // BLOCK, BLOCK, HEADS) * blocks
    return 0.05 * shaped.reshape(TOKENS, HEADS)


def draw_decay_rate(key, part):
    key = jax.random.fold_in(key, 23)
    first_key, second_key, third_key = jax.random.split(key, 3)
    keep_rate = min(0.3, 23.0 / TOKENS)
    lowest_rate = keep_rate * keep_rate / 0.67 * 1.002
    highest_rate = 0.669
    fast_share = 0.5
    chosen = jax.random.uniform(first_key, (HEADS,), jnp.float32) < fast_share
    fast_rate = jnp.exp(jax.random.uniform(second_key, (HEADS,), jnp.float32, math.log(keep_rate), math.log(highest_rate)))
    slow_rate = jnp.exp(jax.random.uniform(third_key, (HEADS,), jnp.float32, math.log(lowest_rate), math.log(keep_rate)))
    return jnp.where(chosen, fast_rate, slow_rate)


def raised(result, key, source, target, parts, factor):
    owner, partner = [(jnp.arange(result.shape[dim]) // (result.shape[dim] // parts)).reshape([-1 if axis == dim else 1 for axis in range(result.ndim)]) for dim in (source, target)]
    chosen = jax.random.permutation(key, parts)[partner]
    strong = (owner == chosen) | (owner == (partner + parts // 2) % parts)
    return jnp.where(strong, factor * result, result)


def level_of(rng, shape, cuts, low, top_value):
    gain, own = 1.0, jax.random.fold_in(rng, 6)
    for axis_at, shards_of in cuts:
        steps = jnp.exp(jax.random.uniform(jax.random.fold_in(own, axis_at), (shards_of,), jnp.float32, low / len(cuts), top_value / len(cuts)))
        gain = gain * jnp.repeat(steps, shape[axis_at] // shards_of).reshape([-1 if axis == axis_at else 1 for axis in range(len(shape))])
    return gain


def centred(key, dims, scale, reach, cuts=(), kind=jnp.bfloat16):
    result = jax.random.normal(key, dims, jnp.float32) * scale
    if len(cuts) > 0:
        result = level_of(key, dims, cuts, -0.22, 0.18) * result
    return jnp.clip(result, min=-reach, max=reach).astype(kind)


def bell_draw_with(key, extent, deviation, bound, cuts, heavy, kind=jnp.bfloat16):
    drawn = deviation * jax.random.normal(key, extent, jnp.float32)
    if cuts:
        drawn = drawn * level_of(key, extent, cuts, -0.22, 0.18)
    return jnp.clip(raised(drawn, jax.random.fold_in(key, 3), *heavy), -bound, bound).astype(kind)


def setup_inputs(seed: int = 0) -> dict:
    splits = jax.random.split(jax.random.key(seed), 12)
    head_values = centred(splits[0], (TOKENS, INNER), 1.0, 6.0, ((0, 32), (1, 4)))
    gate_values = centred(splits[1], (TOKENS, INNER), 1.0, 6.0, ((0, 32), (1, 4)))
    write_keys = centred(splits[2], (TOKENS, STATE), 0.3, 2.0, ((0, 32),))
    read_keys = centred(splits[3], (TOKENS, STATE), 0.3, 2.0, ((0, 32),))
    step_size = draw_step_size(jax.random.fold_in(splits[11], 71), 0)
    decay_rate = draw_decay_rate(jax.random.fold_in(splits[11], 71), 0)
    skip_weight = jnp.clip(0.5 + 1.0 * jax.random.uniform(splits[6], (HEADS,), jnp.float32) ** level_of(splits[6], (HEADS,), ((0, 4),), -0.2, 0.2), 0.5, 1.5)
    prior_state = centred(splits[7], (HEADS, HEAD_DIM, STATE), 1.0, 6.0, ((0, 4),), jnp.float32)
    norm_gain = jnp.clip(1.0 + 0.1 * jax.random.normal(splits[8], (INNER,), jnp.float32), 0.5, 1.5)
    out_weight = bell_draw_with(splits[9], (INNER, D), INNER ** -0.5, 0.125, ((0, 4), (1, 32)), (0, 1, 32, 2.75))
    residual = centred(splits[10], (TOKENS, D), 1.0, 6.0, ((0, 32), (1, 4)))
    return dict(head_values=head_values, gate_values=gate_values, write_keys=write_keys, read_keys=read_keys, step_size=step_size, decay_rate=decay_rate, skip_weight=skip_weight, prior_state=prior_state, norm_gain=norm_gain, out_weight=out_weight, residual=residual)


epsilon = 1e-05

def reference(head_values, gate_values, write_keys, read_keys, step_size, decay_rate, skip_weight, prior_state, norm_gain, out_weight, residual):
    block_count = TOKENS // BLOCK
    by_head = head_values.reshape(block_count, BLOCK, HEADS, HEAD_DIM)
    write_blocks = write_keys.reshape(block_count, BLOCK, STATE)
    read_blocks = read_keys.reshape(block_count, BLOCK, STATE)
    step_blocks = step_size.reshape(block_count, BLOCK, HEADS)
    causal = jnp.arange(BLOCK)[:, None] >= jnp.arange(BLOCK)[None, :]

    def block_step(carry_state, inputs):
        values, writes, reads, steps = inputs
        cumulative = jnp.cumsum(-steps * decay_rate[None, :], axis=0)
        scores = jnp.dot(reads, writes.T, preferred_element_type=jnp.float32)
        spread_log = jnp.where(causal[:, :, None], cumulative[:, None, :] - cumulative[None, :, :], 0.0)
        mixing = jnp.where(causal[:, :, None], jnp.exp(spread_log), 0.0) * scores[:, :, None] * steps[None, :, :]
        mixing = mixing.astype(jnp.bfloat16)
        within = jnp.einsum('tsh,shp->thp', mixing.astype(jnp.float32), values.astype(jnp.float32))
        carried = jnp.exp(cumulative)[:, :, None] * jnp.einsum('tn,hpn->thp', reads.astype(jnp.float32), carry_state, precision=lax.Precision.HIGHEST)
        mixed = within + carried + skip_weight[None, :, None] * values.astype(jnp.float32)
        block_log = cumulative[-1]
        to_end = jnp.exp(block_log[None, :] - cumulative) * steps
        weighted = (values.astype(jnp.float32) * to_end[:, :, None]).astype(jnp.bfloat16)
        local_state = jnp.einsum('thp,tn->hpn', weighted.astype(jnp.float32), writes.astype(jnp.float32))
        next_state = jnp.exp(block_log)[:, None, None] * carry_state + local_state
        return (next_state, mixed)
    final_state, mixed = lax.scan(block_step, prior_state, (by_head, write_blocks, read_blocks, step_blocks))
    mixed = mixed.reshape(TOKENS, INNER)
    gated = mixed * jax.nn.silu(gate_values.astype(jnp.float32))
    square = lax.optimization_barrier(jnp.mean(gated * gated, axis=1))
    normed = (gated * lax.rsqrt(square + epsilon)[:, None] * norm_gain[None, :]).astype(jnp.bfloat16)
    projected = jnp.dot(normed, out_weight, preferred_element_type=jnp.float32)
    return (residual.astype(jnp.float32) + projected).astype(jnp.bfloat16)
```

```python
import functools

import jax
import jax.numpy as jnp
from jax import lax
from jax.experimental import pallas as pl
from jax.experimental.pallas import tpu as pltpu
from jax.sharding import Mesh, PartitionSpec as P

EPSILON = 1e-05
ROWS = 256
HALF = 128
HEADS = 16
WIDTH = 128
LANES = HEADS * WIDTH
SPLIT = LANES // 2
PIECE = 512
INNER = 8192
F32 = jnp.float32
BF16 = jnp.bfloat16
HIGHEST = lax.Precision.HIGHEST
VMEM = pl.BlockSpec(memory_space=pltpu.VMEM)
SMEM = pl.BlockSpec(memory_space=pltpu.SMEM)


def params(mib=32):
    return pltpu.CompilerParams(vmem_limit_bytes=mib * 2**20)


def cost(flops, bytes_accessed, transcendentals=0):
    return pl.CostEstimate(
        flops=flops, bytes_accessed=bytes_accessed, transcendentals=transcendentals
    )


def lower(rows):
    return lax.broadcasted_iota(jnp.int32, (rows, rows), 0) >= lax.broadcasted_iota(
        jnp.int32, (rows, rows), 1
    )


def cumulate(step, rate):
    ones = jnp.where(lower(ROWS), 1.0, 0.0).astype(F32)
    return jnp.dot(ones, -step * rate, precision=HIGHEST, preferred_element_type=F32)


def three(row):
    high = row.astype(BF16)
    rest = row - high.astype(F32)
    middle = rest.astype(BF16)
    last = (rest - middle.astype(F32)).astype(BF16)
    return high.astype(F32), middle.astype(F32), last.astype(F32)


def stack_rows(rows, count):
    width = rows[0].shape[1]
    index = lax.broadcasted_iota(jnp.int32, (count, width), 0)
    result = jnp.zeros((count, width), F32)
    for place, row in enumerate(rows):
        result = jnp.where(index == place, row, result)
    return result


def unpack_rows(block):
    block = block.astype(F32)
    return block[0:1] + block[1:2] + block[2:3]


def state_kernel(place, value_ref, write_ref, step_ref, rate_ref, keep_ref, send_ref, state, logs):
    core = place[0]
    step = step_ref[...]
    cumulative = cumulate(step, rate_ref[...])
    last = cumulative[ROWS - 1 : ROWS]
    to_end = jnp.exp(last - cumulative) * step
    write = write_ref[...].T
    for head in range(HEADS):
        at = slice(head * WIDTH, (head + 1) * WIDTH)
        weighted = (value_ref[:, at].astype(F32) * to_end[:, head : head + 1]).astype(BF16)
        state[:, at] = jnp.dot(write, weighted, preferred_element_type=F32)
        logs[:, at] = jnp.broadcast_to(last[:, head : head + 1], (8, WIDTH))
    mine = pl.ds(pl.multiple_of(core * SPLIT, SPLIT), SPLIT)
    other = pl.ds(pl.multiple_of((1 - core) * SPLIT, SPLIT), SPLIT)
    keep_ref[0:WIDTH, :] = state[:, mine]
    keep_ref[WIDTH:, :] = logs[:, mine]
    send_ref[0:WIDTH, :] = state[:, other]
    send_ref[WIDTH:, :] = logs[:, other]


def local_state(place, values, writes, steps, rate):
    shape = jax.ShapeDtypeStruct((WIDTH + 8, SPLIT), F32)
    return pl.pallas_call(
        state_kernel,
        out_shape=(shape, shape),
        in_specs=[SMEM] + [VMEM] * 4,
        out_specs=(VMEM, VMEM),
        scratch_shapes=[pltpu.VMEM((WIDTH, LANES), F32), pltpu.VMEM((8, LANES), F32)],
        compiler_params=params(),
        cost_estimate=cost(2 * WIDTH * ROWS * LANES, 3 * 2**20),
        name="local_state",
    )(place, values, writes, steps, rate)


def plain_kernel(
    value_ref, gate_ref, write_ref, read_ref, step_ref, rate_ref, skip_ref, plain_ref, scale_ref
):
    step = step_ref[...]
    cumulative = cumulate(step, rate_ref[...])
    across = cumulative.T
    step_across = step.T
    decay = jnp.exp(cumulative)
    scores = lax.dot_general(
        read_ref[...], write_ref[...], (((1,), (1,)), ((), ())), preferred_element_type=F32
    )
    scores = jnp.where(lower(ROWS), scores, 0.0)
    for head in range(HEADS):
        at = slice(head * WIDTH, (head + 1) * WIDTH)
        spread = jnp.minimum(cumulative[:, head : head + 1] - across[head : head + 1, :], 0.0)
        mixing = (jnp.exp(spread) * scores * step_across[head : head + 1, :]).astype(BF16)
        value = value_ref[:, at]
        within = jnp.dot(mixing, value, preferred_element_type=F32)
        within = within + skip_ref[:, head : head + 1] * value.astype(F32)
        gate = gate_ref[:, at].astype(F32)
        gate = gate / (1.0 + jnp.exp(-gate))
        plain_ref[:, at] = within * gate
        scale_ref[:, at] = decay[:, head : head + 1] * gate


def plain_part(values, gates, writes, reads, steps, rate, skip):
    shape = jax.ShapeDtypeStruct((ROWS, LANES), F32)
    return pl.pallas_call(
        plain_kernel,
        out_shape=(shape, shape),
        in_specs=[VMEM] * 7,
        out_specs=(VMEM, VMEM),
        compiler_params=params(),
        cost_estimate=cost(
            2 * ROWS * ROWS * LANES, 7 * 2**20, HEADS * ROWS * ROWS + ROWS * LANES
        ),
        name="plain_part",
    )(values, gates, writes, reads, steps, rate, skip)


def turn_kernel(place, prior_ref, out_ref):
    out_ref[...] = prior_ref[0].T


def turned_prior(place, prior):
    heads = HEADS // 2
    return pl.pallas_call(
        turn_kernel,
        grid_spec=pltpu.PrefetchScalarGridSpec(
            num_scalar_prefetch=1,
            grid=(heads,),
            in_specs=[
                pl.BlockSpec((1, WIDTH, WIDTH), lambda i, place: (place[0] * heads + i, 0, 0))
            ],
            out_specs=pl.BlockSpec((WIDTH, WIDTH), lambda i, place: (0, i)),
        ),
        out_shape=jax.ShapeDtypeStruct((WIDTH, SPLIT), F32),
        compiler_params=params(),
        cost_estimate=cost(0, 2**20),
        name="turned_prior",
    )(place, prior)


MESSAGE = jax.ShapeDtypeStruct((WIDTH + 16, SPLIT), BF16)


def write_message(out_ref, state, log):
    out_ref[0:WIDTH, :] = state.astype(BF16)
    out_ref[WIDTH:, :] = stack_rows(three(log), 16).astype(BF16)


def ordered(core, keep_ref, got_ref):
    kept, got = keep_ref[...], got_ref[...]
    first = jnp.where(core == 0, kept, got)
    second = jnp.where(core == 0, got, kept)
    split = lambda part: (part[0:WIDTH], part[WIDTH : WIDTH + 1])
    return split(first), split(second)


def chip_kernel(place, keep_ref, got_ref, out_ref):
    (state0, log0), (state1, log1) = ordered(place[0], keep_ref, got_ref)
    write_message(out_ref, jnp.exp(log1) * state0 + state1, log0 + log1)


def chip_total(place, keep, got):
    return pl.pallas_call(
        chip_kernel,
        out_shape=MESSAGE,
        in_specs=[SMEM] + [VMEM] * 2,
        out_specs=VMEM,
        compiler_params=params(),
        cost_estimate=cost(2 * WIDTH * SPLIT, 2**20),
        name="chip_total",
    )(place, keep, got)


def fold(here, parts, whole):
    logs = [unpack_rows(part[WIDTH : WIDTH + 16, :]) for part in parts]
    at = [lax.rem(here - k + 4, 4) for k in range(4)]
    total = None
    for k in range(4):
        if not whole and k == 0:
            continue
        after = jnp.zeros_like(logs[0])
        for j in range(4):
            if j == k or (not whole and j == 0):
                continue
            counts = at[j] > at[k]
            if not whole:
                counts = jnp.logical_and(counts, at[j] < here)
            after = after + jnp.where(counts, logs[j], 0.0)
        weight = jnp.exp(after)
        if not whole:
            weight = jnp.where(at[k] < here, weight, 0.0)
        term = weight * parts[k][0:WIDTH, :].astype(F32)
        total = term if total is None else total + term
    log = jnp.zeros_like(logs[0])
    for k in range(4):
        if whole:
            log = log + logs[k]
        elif k:
            log = log + jnp.where(at[k] < here, logs[k], 0.0)
    return total, log


def row_kernel(place, p0, p1, p2, p3, out_ref, before_ref):
    parts = (p0, p1, p2, p3)
    total, log = fold(place[2], parts, True)
    write_message(out_ref, total, log)
    total, log = fold(place[2], parts, False)
    before_ref[0:WIDTH, :] = total
    before_ref[WIDTH:, :] = jnp.broadcast_to(log, (8, SPLIT))


def row_total(place, parts):
    return pl.pallas_call(
        row_kernel,
        out_shape=(MESSAGE, jax.ShapeDtypeStruct((WIDTH + 8, SPLIT), F32)),
        in_specs=[SMEM] + [VMEM] * 4,
        out_specs=(VMEM, VMEM),
        compiler_params=params(),
        cost_estimate=cost(16 * WIDTH * SPLIT, 2 * 2**20),
        name="row_total",
    )(place, *parts)


def enter_kernel(
    place, p0, p1, p2, p3, before_ref, prior_ref, keep_ref, got_ref, mine_ref, other_ref
):
    core = place[0]
    total, log = fold(place[3], (p0, p1, p2, p3), False)
    entering = total + jnp.exp(log) * prior_ref[...]
    entering = jnp.exp(before_ref[WIDTH : WIDTH + 1, :]) * entering + before_ref[0:WIDTH, :]
    (state0, log0), _ = ordered(core, keep_ref, got_ref)
    second = jnp.exp(log0) * entering + state0
    mine_ref[...] = jnp.where(core == 0, entering, second).astype(BF16)
    other_ref[...] = jnp.where(core == 0, second, entering).astype(BF16)


def entering_state(place, parts, before, prior, keep, got):
    shape = jax.ShapeDtypeStruct((WIDTH, SPLIT), BF16)
    return pl.pallas_call(
        enter_kernel,
        out_shape=(shape, shape),
        in_specs=[SMEM] + [VMEM] * 8,
        out_specs=(VMEM, VMEM),
        compiler_params=params(),
        cost_estimate=cost(16 * WIDTH * SPLIT, 4 * 2**20),
        name="entering_state",
    )(place, *parts, before, prior, keep, got)


def gated_kernel(
    place, mine_ref, other_ref, read_ref, plain_ref, scale_ref, gain_ref, top_ref, low_ref, stat_ref, acc
):
    step = pl.program_id(0)
    mine = place[0] == step // 2
    entering = jnp.where(mine, mine_ref[...], other_ref[...])
    carried = jnp.dot(read_ref[...], entering, preferred_element_type=F32)
    gated = plain_ref[...] + scale_ref[...] * carried
    result = (gated * gain_ref[...]).astype(BF16)
    top_ref[...] = result[:HALF]
    low_ref[...] = result[HALF:]
    square = gated * gated
    part = square[:, 0:128]
    for at in range(128, square.shape[1], 128):
        part = part + square[:, at : at + 128]

    @pl.when(step == 0)
    def _():
        acc[...] = part

    @pl.when(step > 0)
    def _():
        acc[...] += part

    @pl.when(step == pl.num_programs(0) - 1)
    def _():
        row = jnp.sum(acc[...].T, axis=0, keepdims=True)
        stat_ref[...] = jnp.zeros_like(stat_ref)
        stat_ref[:, 0:ROWS] = stack_rows(three(row), 16).astype(BF16)


def gated_part(place, mine, other, reads, plain, scale, gain):
    steps = 4
    width = LANES // steps
    half = pl.BlockSpec((HALF, width), lambda i, place: (0, i))
    wide = pl.BlockSpec((ROWS, width), lambda i, place: (0, i))
    state = pl.BlockSpec((WIDTH, width), lambda i, place: (0, lax.rem(i, 2)))
    whole = lambda shape: pl.BlockSpec(shape, lambda i, place: (0, 0))
    return pl.pallas_call(
        gated_kernel,
        grid_spec=pltpu.PrefetchScalarGridSpec(
            num_scalar_prefetch=1,
            grid=(steps,),
            in_specs=[
                state,
                state,
                whole((ROWS, WIDTH)),
                wide,
                wide,
                pl.BlockSpec((1, width), lambda i, place: (0, i)),
            ],
            out_specs=[half, half, whole((16, PIECE))],
            scratch_shapes=[pltpu.VMEM((ROWS, 128), F32)],
        ),
        out_shape=(
            jax.ShapeDtypeStruct((HALF, LANES), BF16),
            jax.ShapeDtypeStruct((HALF, LANES), BF16),
            jax.ShapeDtypeStruct((16, PIECE), BF16),
        ),
        compiler_params=params(),
        cost_estimate=cost(2 * ROWS * WIDTH * LANES, 6 * 2**20),
        name="gated_part",
    )(place, mine, other, reads, plain, scale, gain)


def project_kernel(place, top_ref, low_ref, weight_ref, *refs):
    stats = refs[:-4]
    step = pl.program_id(0)
    for k, out_ref in enumerate(refs[-4:]):

        @pl.when(step == k)
        def _(out_ref=out_ref):
            for core in range(2):
                at = slice(core * 256, (core + 1) * 256)
                weight = weight_ref[core]
                for rows, ref in ((0, top_ref), (HALF, low_ref)):
                    out_ref[rows : rows + HALF, at] = jnp.dot(
                        ref[...], weight, preferred_element_type=F32
                    ).astype(BF16)
            for stat in stats:
                out_ref[ROWS:, :] = stat[...]


def project(place, top, low, weight, stats=None):
    rows = ROWS if stats is None else ROWS + 16
    extra = () if stats is None else (stats,)
    half = pl.BlockSpec((HALF, LANES), lambda i, place: (0, 0))
    out = pl.BlockSpec((rows, PIECE), lambda i, place: (0, 0))
    return pl.pallas_call(
        project_kernel,
        grid_spec=pltpu.PrefetchScalarGridSpec(
            num_scalar_prefetch=1,
            grid=(4,),
            in_specs=[
                half,
                half,
                pl.BlockSpec(
                    (2, LANES, 256), lambda i, place: (lax.rem(place[1] + i, 4), 0, 0)
                ),
            ]
            + [pl.BlockSpec((16, PIECE), lambda i, place: (0, 0))] * len(extra),
            out_specs=[out] * 4,
        ),
        out_shape=[jax.ShapeDtypeStruct((rows, PIECE), BF16)] * 4,
        compiler_params=params(),
        cost_estimate=cost(2 * ROWS * LANES * 4 * PIECE, 10 * 2**20),
        name="project",
    )(place, top, low, weight, *extra)


def add(parts, rows):
    total = parts[0][rows, :].astype(F32)
    for part in parts[1:]:
        total = total + part[rows, :].astype(F32)
    return total


def sums_kernel(*refs):
    first, second, (down_ref, up_ref) = refs[0:4], refs[4:8], refs[8:]
    for at, parts in ((0, first), (HALF, second)):
        down_ref[at : at + HALF, :] = add(parts, slice(0, HALF)).astype(BF16)
        up_ref[at : at + HALF, :] = add(parts, slice(HALF, ROWS)).astype(BF16)


def neighbour_sums(first, second):
    shape = jax.ShapeDtypeStruct((ROWS, PIECE), BF16)
    return pl.pallas_call(
        sums_kernel,
        out_shape=(shape, shape),
        in_specs=[VMEM] * 8,
        out_specs=(VMEM, VMEM),
        compiler_params=params(),
        cost_estimate=cost(8 * ROWS * PIECE, 10 * ROWS * PIECE * 2),
        name="neighbour_sums",
    )(*first, *second)


def sum_kernel(*refs):
    refs[4][...] = add(refs[0:4], slice(0, ROWS)).astype(BF16)


def far_sums(parts):
    return pl.pallas_call(
        sum_kernel,
        out_shape=jax.ShapeDtypeStruct((ROWS, PIECE), BF16),
        in_specs=[VMEM] * 4,
        out_specs=VMEM,
        compiler_params=params(),
        cost_estimate=cost(4 * ROWS * PIECE, 5 * ROWS * PIECE * 2),
        name="far_sums",
    )(*parts)


def finish_kernel(place, p0, p1, p2, p3, up_ref, far_ref, down_ref, residual_ref, out_ref):
    own = (p0, p1, p2, p3)
    square = sum(unpack_rows(part[ROWS : ROWS + 16, 0:ROWS]) for part in own)
    row = lax.rsqrt(square / INNER + EPSILON)
    scale = jnp.broadcast_to(row, (128, ROWS)).T
    step = pl.program_id(0)

    def write(total):
        for at in range(0, PIECE, 128):
            cols = slice(at, at + 128)
            out_ref[:, cols] = (residual_ref[:, cols].astype(F32) + scale * total[:, cols]).astype(
                BF16
            )

    @pl.when(step == 0)
    def _():
        write(add(own, slice(0, ROWS)))

    for k, ref in ((1, up_ref), (2, far_ref), (3, down_ref)):

        @pl.when(step == k)
        def _(ref=ref):
            write(ref[...].astype(F32))


def finish(place, own, up, far, down, residual):
    whole = lambda rows: pl.BlockSpec((rows, PIECE), lambda i, place: (0, 0))
    block = pl.BlockSpec((ROWS, PIECE), lambda i, place: (0, lax.rem(place[2] + i, 4)))
    return pl.pallas_call(
        finish_kernel,
        grid_spec=pltpu.PrefetchScalarGridSpec(
            num_scalar_prefetch=1,
            grid=(4,),
            in_specs=[whole(ROWS + 16)] * 4 + [whole(ROWS)] * 3 + [block],
            out_specs=block,
        ),
        out_shape=jax.ShapeDtypeStruct((ROWS, 4 * PIECE), BF16),
        compiler_params=params(),
        cost_estimate=cost(4 * ROWS * 4 * PIECE, 4 * 2**20),
        name="finish",
    )(place, *own, up, far, down, residual)


def shift(value, axis, by):
    return lax.ppermute(value, axis, [(i, (i + by) % 4) for i in range(4)])


def swap(value):
    return lax.ppermute(value, "core", [(0, 1), (1, 0)])


def scatter(pieces):
    return [pieces[0]] + [shift(pieces[k], "x", k) for k in (1, 2, 3)]


def body(
    head_values,
    gate_values,
    write_keys,
    read_keys,
    step_size,
    decay_rate,
    skip_weight,
    prior_state,
    norm_gain,
    out_weight,
    residual,
):
    place = jnp.stack([lax.axis_index(name) for name in ("core", "x", "y", "z")]).astype(jnp.int32)
    weight = lax.all_gather(out_weight, ("z", "core"))
    rate = decay_rate[None, :]

    keep, send = local_state(place, head_values, write_keys, step_size, rate)
    got = swap(send)
    plain, scale = plain_part(
        head_values, gate_values, write_keys, read_keys, step_size, rate, skip_weight[None, :]
    )
    prior = turned_prior(place, prior_state)
    chip = chip_total(place, keep, got)
    row, before = row_total(place, [chip] + [shift(chip, "y", k) for k in (1, 2, 3)])
    mine, other = entering_state(
        place, [row] + [shift(row, "z", k) for k in (1, 2, 3)], before, prior, keep, got
    )
    other = swap(other)
    top, low, stats = gated_part(place, mine, other, read_keys, plain, scale, norm_gain[None, :])

    top_below, top_above = shift(top, "y", 1), shift(top, "y", -1)
    low_below, low_above = shift(low, "y", 1), shift(low, "y", -1)
    top_far, low_far = shift(top_below, "y", 1), shift(low_above, "y", -1)

    own = scatter(project(place, top, low, weight, stats))
    first = scatter(project(place, top_below, top_above, weight))
    second = scatter(project(place, low_below, low_above, weight))
    far = scatter(project(place, top_far, low_far, weight))

    down, up = neighbour_sums(first, second)
    from_above = shift(down, "y", -1)
    from_below = shift(up, "y", 1)
    from_far = shift(far_sums(far), "y", 2)
    return finish(place, own, from_above, from_far, from_below, residual)


def solution(mesh):
    grid = Mesh(mesh.devices.reshape(4, 4, 2, 4), ("z", "y", "core", "x"))
    ctx = ("z", "y", "core")
    in_specs = (
        P(ctx, "x"),
        P(ctx, "x"),
        P(ctx, None),
        P(ctx, None),
        P(ctx, "x"),
        P("x"),
        P("x"),
        P("x", None, None),
        P("x"),
        P("x", ctx),
        P(ctx, "x"),
    )
    return jax.shard_map(
        body, mesh=grid, in_specs=in_specs, out_specs=P(ctx, "x"), check_vma=False
    )
```

```python
import functools

import jax
import jax.numpy as jnp
from jax import lax
from jax.experimental import pallas as pl
from jax.experimental.pallas import tpu as pltpu
from jax.sharding import Mesh, PartitionSpec as P

EPSILON = 1e-05
ROWS = 256
HALF = 128
HEADS = 16
WIDTH = 128
LANES = HEADS * WIDTH
SLICE = LANES // 8
SPLIT = LANES // 2
PIECE = 512
INNER = 8192
F32 = jnp.float32
BF16 = jnp.bfloat16
HIGHEST = lax.Precision.HIGHEST
VMEM = pl.BlockSpec(memory_space=pltpu.VMEM)
SMEM = pl.BlockSpec(memory_space=pltpu.SMEM)


def params(mib=16):
    return pltpu.CompilerParams(vmem_limit_bytes=mib * 2**20)


ANY = pl.BlockSpec(memory_space=pl.ANY)


def cost(flops, bytes_accessed, transcendentals=0):
    return pl.CostEstimate(
        flops=flops, bytes_accessed=bytes_accessed, transcendentals=transcendentals
    )


def lower(rows):
    return lax.broadcasted_iota(jnp.int32, (rows, rows), 0) >= lax.broadcasted_iota(
        jnp.int32, (rows, rows), 1
    )


def cumulate(step, rate):
    ones = jnp.where(lower(ROWS), 1.0, 0.0).astype(F32)
    column = jnp.broadcast_to(rate, (8, HEADS)).T[:, 0:1]
    return lax.dot_general(
        -step * column,
        ones,
        (((1,), (1,)), ((), ())),
        precision=HIGHEST,
        preferred_element_type=F32,
    )


def three(row):
    high = row.astype(BF16)
    rest = row - high.astype(F32)
    middle = rest.astype(BF16)
    last = (rest - middle.astype(F32)).astype(BF16)
    return high.astype(F32), middle.astype(F32), last.astype(F32)


def stack_rows(rows, count):
    width = rows[0].shape[1]
    index = lax.broadcasted_iota(jnp.int32, (count, width), 0)
    result = jnp.zeros((count, width), F32)
    for place, row in enumerate(rows):
        result = jnp.where(index == place, row, result)
    return result


def unpack_rows(block):
    block = block.astype(F32)
    return block[0:1] + block[1:2] + block[2:3]


def state_kernel(place, value_ref, write_ref, step_ref, rate_ref, keep_ref, send_ref, state, logs):
    core = place[0]
    step = step_ref[...]
    across = cumulate(step, rate_ref[...])
    to_end = (jnp.exp(across[:, ROWS - 1 : ROWS] - across) * step).T
    last = across.T[ROWS - 1 : ROWS]
    write = write_ref[...].T
    for head in range(HEADS):
        at = slice(head * WIDTH, (head + 1) * WIDTH)
        weighted = (value_ref[:, at].astype(F32) * to_end[:, head : head + 1]).astype(BF16)
        state[:, at] = jnp.dot(write, weighted, preferred_element_type=F32)
        logs[:, at] = jnp.broadcast_to(last[:, head : head + 1], (8, WIDTH))
    mine = pl.ds(pl.multiple_of(core * SPLIT, SPLIT), SPLIT)
    other = pl.ds(pl.multiple_of((1 - core) * SPLIT, SPLIT), SPLIT)
    keep_ref[0:WIDTH, :] = state[:, mine]
    keep_ref[WIDTH:, :] = logs[:, mine]
    send_ref[0:WIDTH, :] = state[:, other]
    send_ref[WIDTH:, :] = logs[:, other]


def whole(shape):
    return pl.BlockSpec(shape, lambda i, place: (0,) * len(shape))


def local_state(place, values, writes, steps, rate):
    shape = (WIDTH + 8, SPLIT)
    return pl.pallas_call(
        state_kernel,
        grid_spec=pltpu.PrefetchScalarGridSpec(
            num_scalar_prefetch=1,
            grid=(1,),
            in_specs=[whole(part.shape) for part in (values, writes, steps, rate)],
            out_specs=[whole(shape), whole(shape)],
            scratch_shapes=[pltpu.VMEM((WIDTH, LANES), F32), pltpu.VMEM((8, LANES), F32)],
        ),
        out_shape=[jax.ShapeDtypeStruct(shape, F32)] * 2,
        compiler_params=params(48),
        cost_estimate=cost(2 * WIDTH * ROWS * LANES, 3 * 2**20),
        name="local_state",
    )(place, values, writes, steps, rate)


def plain_kernel(
    value_ref, gate_ref, write_ref, read_ref, step_ref, rate_ref, skip_ref, _, plain_ref, scale_ref
):
    step = step_ref[...]
    across = cumulate(step, rate_ref[...])
    cumulative = across.T
    decay = jnp.exp(cumulative)
    scores = lax.dot_general(
        read_ref[...], write_ref[...], (((1,), (1,)), ((), ())), preferred_element_type=F32
    )
    scores = jnp.where(lower(ROWS), scores, 0.0)
    for head in range(HEADS):
        at = slice(head * WIDTH, (head + 1) * WIDTH)
        spread = jnp.minimum(cumulative[:, head : head + 1] - across[head : head + 1, :], 0.0)
        mixing = (jnp.exp(spread) * scores * step[head : head + 1, :]).astype(BF16)
        value = value_ref[:, at]
        within = jnp.dot(mixing, value, preferred_element_type=F32)
        within = within + skip_ref[:, head : head + 1] * value.astype(F32)
        gate = gate_ref[:, at].astype(F32)
        gate = gate / (1.0 + jnp.exp(-gate))
        plain_ref[:, at] = within * gate
        scale_ref[:, at] = decay[:, head : head + 1] * gate


def plain_part(values, gates, writes, reads, steps, rate, skip, after):
    shape = jax.ShapeDtypeStruct((ROWS, LANES), F32)
    return pl.pallas_call(
        plain_kernel,
        out_shape=(shape, shape),
        in_specs=[VMEM] * 7 + [ANY],
        out_specs=(VMEM, VMEM),
        compiler_params=params(),
        cost_estimate=cost(
            2 * ROWS * ROWS * LANES, 7 * 2**20, HEADS * ROWS * ROWS + ROWS * LANES
        ),
        name="plain_part",
    )(values, gates, writes, reads, steps, rate, skip, after)


def turn_kernel(place, prior_ref, _, out_ref):
    out_ref[...] = prior_ref[0].T


def turned_prior(place, prior, after):
    heads = 2
    first = lambda place: 4 * place[0] + place[2]
    return pl.pallas_call(
        turn_kernel,
        grid_spec=pltpu.PrefetchScalarGridSpec(
            num_scalar_prefetch=1,
            grid=(heads,),
            in_specs=[
                pl.BlockSpec((1, WIDTH, WIDTH), lambda i, place: (first(place) * heads + i, 0, 0)),
                ANY,
            ],
            out_specs=pl.BlockSpec((WIDTH, WIDTH), lambda i, place: (0, i)),
        ),
        out_shape=jax.ShapeDtypeStruct((WIDTH, SLICE), F32),
        compiler_params=params(),
        cost_estimate=cost(0, 2**20),
        name="turned_prior",
    )(place, prior, after)


MESSAGE = jax.ShapeDtypeStruct((WIDTH + 16, SLICE), BF16)


def write_message(out_ref, state, log):
    out_ref[0:WIDTH, :] = state.astype(BF16)
    out_ref[WIDTH:, :] = stack_rows(three(log), 16).astype(BF16)


def slice_of(place, k):
    return pl.ds(pl.multiple_of(lax.rem(place[2] + k + 4, 4) * SLICE, SLICE), SLICE)


def chip_kernel(place, keep_ref, got_ref, *refs):
    outs, total, logs = refs[:4], refs[4], refs[5]
    first = place[0] == 0
    kept, got = keep_ref[...], got_ref[...]
    state0 = jnp.where(first, kept, got)
    state1 = jnp.where(first, got, kept)
    log1 = state1[WIDTH : WIDTH + 1]
    total[...] = jnp.exp(log1) * state0[0:WIDTH] + state1[0:WIDTH]
    logs[...] = state0[WIDTH:] + state1[WIDTH:]
    for k, out_ref in enumerate(outs):
        at = slice_of(place, k)
        write_message(out_ref, total[:, at], logs[0:1, at])


def chip_total(place, keep, got):
    pieces = pl.pallas_call(
        chip_kernel,
        out_shape=[MESSAGE] * 4,
        in_specs=[SMEM] + [VMEM] * 2,
        out_specs=[VMEM] * 4,
        scratch_shapes=[pltpu.VMEM((WIDTH, SPLIT), F32), pltpu.VMEM((8, SPLIT), F32)],
        compiler_params=params(),
        cost_estimate=cost(2 * WIDTH * SPLIT, 2**20),
        name="chip_total",
    )(place, keep, got)
    return list(pieces)


def fold(here, parts, before):
    logs = [unpack_rows(part[WIDTH : WIDTH + 16, :]) for part in parts]
    at = [lax.rem(here - k + 4, 4) for k in range(4)]
    total = jnp.zeros((WIDTH, SLICE), F32)
    log = jnp.zeros_like(logs[0])
    for k in range(4):
        after = jnp.zeros_like(log)
        for j in range(4):
            if j != k:
                counts = jnp.logical_and(at[j] > at[k], at[j] < before)
                after = after + jnp.where(counts, logs[j], 0.0)
        weight = jnp.where(at[k] < before, jnp.exp(after), 0.0)
        total = total + weight * parts[k][0:WIDTH, :].astype(F32)
        log = log + jnp.where(at[k] < before, logs[k], 0.0)
    return total, log


def row_kernel(place, p0, p1, p2, p3, _plain, _prior, out_ref, before_ref):
    parts = (p0, p1, p2, p3)
    write_message(out_ref, *fold(place[2], parts, 4))
    for k in range(4):
        total, log = fold(place[2], parts, lax.rem(place[2] + k, 4))
        before_ref[k, 0:WIDTH, :] = total
        before_ref[k, WIDTH:, :] = jnp.broadcast_to(log, (8, SLICE))


def row_total(place, parts, after):
    return pl.pallas_call(
        row_kernel,
        out_shape=(MESSAGE, jax.ShapeDtypeStruct((4, WIDTH + 8, SLICE), F32)),
        in_specs=[SMEM] + [VMEM] * 4 + [ANY] * 2,
        out_specs=(VMEM, VMEM),
        compiler_params=params(),
        cost_estimate=cost(40 * WIDTH * SLICE, 2**20),
        name="row_total",
    )(place, *parts, *after)


def row_enter_kernel(place, p0, p1, p2, p3, before_ref, prior_ref, *refs):
    total, log = fold(place[3], (p0, p1, p2, p3), place[3])
    entering = total + jnp.exp(log) * prior_ref[...]
    for k, out_ref in enumerate(refs[-4:]):
        decay = jnp.exp(before_ref[k, WIDTH : WIDTH + 1, :])
        out_ref[...] = (decay * entering + before_ref[k, 0:WIDTH, :]).astype(BF16)


def row_enter(place, parts, before, prior, after):
    pieces = pl.pallas_call(
        row_enter_kernel,
        out_shape=[jax.ShapeDtypeStruct((WIDTH, SLICE), BF16)] * 4,
        in_specs=[SMEM] + [VMEM] * 6 + [ANY] * len(after),
        out_specs=[VMEM] * 4,
        compiler_params=params(),
        cost_estimate=cost(16 * WIDTH * SLICE, 2**20),
        name="row_enter",
    )(place, *parts, before, prior, *after)
    return list(pieces)


def enter_kernel(place, p0, p1, p2, p3, keep_ref, got_ref, mine_ref, other_ref, chip):
    first = place[0] == 0
    for k, part in enumerate((p0, p1, p2, p3)):
        chip[:, slice_of(place, -k)] = part[...].astype(F32)
    entering = chip[...]
    state0 = jnp.where(first, keep_ref[...], got_ref[...])
    second = jnp.exp(state0[WIDTH : WIDTH + 1]) * entering + state0[0:WIDTH]
    mine_ref[...] = jnp.where(first, entering, second).astype(BF16)
    other_ref[...] = jnp.where(first, second, entering).astype(BF16)


def entering_state(place, parts, keep, got):
    shape = jax.ShapeDtypeStruct((WIDTH, SPLIT), BF16)
    return pl.pallas_call(
        enter_kernel,
        out_shape=(shape, shape),
        in_specs=[SMEM] + [VMEM] * 6,
        out_specs=(VMEM, VMEM),
        scratch_shapes=[pltpu.VMEM((WIDTH, SPLIT), F32)],
        compiler_params=params(),
        cost_estimate=cost(8 * WIDTH * SPLIT, 2 * 2**20),
        name="entering_state",
    )(place, *parts, keep, got)


def gated_kernel(
    place, mine_ref, other_ref, read_ref, plain_ref, scale_ref, gain_ref, top_ref, low_ref, stat_ref, acc
):
    step = pl.program_id(0)
    mine = place[0] == step // 2
    entering = jnp.where(mine, mine_ref[...], other_ref[...])
    carried = jnp.dot(read_ref[...], entering, preferred_element_type=F32)
    gated = plain_ref[...] + scale_ref[...] * carried
    result = (gated * gain_ref[...]).astype(BF16)
    top_ref[...] = result[:HALF]
    low_ref[...] = result[HALF:]
    square = gated * gated
    part = square[:, 0:128]
    for at in range(128, square.shape[1], 128):
        part = part + square[:, at : at + 128]

    @pl.when(step == 0)
    def _():
        acc[...] = part

    @pl.when(step > 0)
    def _():
        acc[...] += part

    @pl.when(step == pl.num_programs(0) - 1)
    def _():
        row = jnp.sum(acc[...].T, axis=0, keepdims=True)
        stat_ref[...] = jnp.zeros_like(stat_ref)
        stat_ref[:, 0:ROWS] = stack_rows(three(row), 16).astype(BF16)


def gated_part(place, mine, other, reads, plain, scale, gain):
    steps = 4
    width = LANES // steps
    half = pl.BlockSpec((HALF, width), lambda i, place: (0, i))
    wide = pl.BlockSpec((ROWS, width), lambda i, place: (0, i))
    state = pl.BlockSpec((WIDTH, width), lambda i, place: (0, lax.rem(i, 2)))
    return pl.pallas_call(
        gated_kernel,
        grid_spec=pltpu.PrefetchScalarGridSpec(
            num_scalar_prefetch=1,
            grid=(steps,),
            in_specs=[
                state,
                state,
                whole((ROWS, WIDTH)),
                wide,
                wide,
                pl.BlockSpec((1, width), lambda i, place: (0, i)),
            ],
            out_specs=[half, half, whole((16, PIECE))],
            scratch_shapes=[pltpu.VMEM((ROWS, 128), F32)],
        ),
        out_shape=(
            jax.ShapeDtypeStruct((HALF, LANES), BF16),
            jax.ShapeDtypeStruct((HALF, LANES), BF16),
            jax.ShapeDtypeStruct((16, PIECE), BF16),
        ),
        compiler_params=params(),
        cost_estimate=cost(2 * ROWS * WIDTH * LANES, 6 * 2**20),
        name="gated_part",
    )(place, mine, other, reads, plain, scale, gain)


def project_kernel(has_stats, place, top_ref, low_ref, *refs):
    core, x, z = place[0], place[1], place[3]
    outs = refs[-4:]
    sides = (refs[0:5], refs[5:10])
    depth = LANES // 2
    left = jnp.concatenate([top_ref[...], low_ref[...]], axis=0)
    for j in range(4):
        k = lax.rem(z - x + j + 4, 4)
        for side in range(2):
            own, above, below, first, second = sides[side]
            at = pl.ds(pl.multiple_of(256 * (core if side == 0 else 1 - core), 256), 256)
            if j == 2:
                total = jnp.dot(left[:, :depth], first[...], preferred_element_type=F32)
                total += jnp.dot(left[:, depth:], second[...], preferred_element_type=F32)
            else:
                weight = {0: own, 1: above, 3: below}[j]
                total = jnp.dot(left, weight[...], preferred_element_type=F32)
            total = total.astype(BF16)
            for place_k, out_ref in enumerate(outs):

                @pl.when(k == place_k)
                def _(out_ref=out_ref, at=at, total=total):
                    out_ref[0:ROWS, at] = total

    if has_stats:
        for out_ref in outs:
            out_ref[ROWS:, :] = refs[10][...]


def project(place, top, low, weights, stats=None, after=()):
    rows = ROWS if stats is None else ROWS + 16
    extra = () if stats is None else (stats,)
    pieces = pl.pallas_call(
        functools.partial(project_kernel, stats is not None),
        in_specs=[SMEM] + [VMEM] * (12 + len(extra)) + [ANY] * len(after),
        out_specs=[VMEM] * 4,
        out_shape=[jax.ShapeDtypeStruct((rows, PIECE), BF16)] * 4,
        compiler_params=params(24),
        cost_estimate=cost(2 * ROWS * LANES * 4 * PIECE, 10 * 2**20),
        name="project",
    )(place, top, low, *weights, *extra, *after)
    return list(pieces)


def add(parts, rows):
    total = parts[0][rows, :].astype(F32)
    for part in parts[1:]:
        total = total + part[rows, :].astype(F32)
    return total


def sums_kernel(*refs):
    first, second, (down_ref, up_ref) = refs[0:4], refs[4:8], refs[8:]
    for at, parts in ((0, first), (HALF, second)):
        down_ref[at : at + HALF, :] = add(parts, slice(0, HALF)).astype(BF16)
        up_ref[at : at + HALF, :] = add(parts, slice(HALF, ROWS)).astype(BF16)


def neighbour_sums(first, second):
    shape = jax.ShapeDtypeStruct((ROWS, PIECE), BF16)
    return pl.pallas_call(
        sums_kernel,
        out_shape=(shape, shape),
        in_specs=[VMEM] * 8,
        out_specs=(VMEM, VMEM),
        compiler_params=params(),
        cost_estimate=cost(8 * ROWS * PIECE, 10 * ROWS * PIECE * 2),
        name="neighbour_sums",
    )(*first, *second)


def sum_kernel(*refs):
    refs[4][...] = add(refs[0:4], slice(0, ROWS)).astype(BF16)


def far_sums(parts):
    return pl.pallas_call(
        sum_kernel,
        out_shape=jax.ShapeDtypeStruct((ROWS, PIECE), BF16),
        in_specs=[VMEM] * 4,
        out_specs=VMEM,
        compiler_params=params(),
        cost_estimate=cost(4 * ROWS * PIECE, 5 * ROWS * PIECE * 2),
        name="far_sums",
    )(*parts)


def finish_kernel(place, p0, p1, p2, p3, up_ref, far_ref, down_ref, residual_ref, out_ref):
    own = (p0, p1, p2, p3)
    square = sum(unpack_rows(part[ROWS : ROWS + 16, 0:ROWS]) for part in own)
    row = lax.rsqrt(square / INNER + EPSILON)
    scale = jnp.broadcast_to(row, (128, ROWS)).T
    step = pl.program_id(0)

    def write(total):
        for at in range(0, PIECE, 128):
            cols = slice(at, at + 128)
            out_ref[:, cols] = (residual_ref[:, cols].astype(F32) + scale * total[:, cols]).astype(
                BF16
            )

    @pl.when(step == 0)
    def _():
        write(add(own, slice(0, ROWS)))

    for k, ref in ((1, up_ref), (2, far_ref), (3, down_ref)):

        @pl.when(step == k)
        def _(ref=ref):
            write(ref[...].astype(F32))


def finish(place, own, up, far, down, residual):
    block = pl.BlockSpec((ROWS, PIECE), lambda i, place: (0, lax.rem(place[2] + i, 4)))
    return pl.pallas_call(
        finish_kernel,
        grid_spec=pltpu.PrefetchScalarGridSpec(
            num_scalar_prefetch=1,
            grid=(4,),
            in_specs=[whole((ROWS + 16, PIECE))] * 4 + [whole((ROWS, PIECE))] * 3 + [block],
            out_specs=block,
        ),
        out_shape=jax.ShapeDtypeStruct((ROWS, 4 * PIECE), BF16),
        compiler_params=params(),
        cost_estimate=cost(4 * ROWS * 4 * PIECE, 4 * 2**20),
        name="finish",
    )(place, *own, up, far, down, residual)


def shift(value, axis, by):
    return lax.ppermute(value, axis, [(i, (i + by) % 4) for i in range(4)])


def swap(value):
    return lax.ppermute(value, "core", [(0, 1), (1, 0)])


def later(values, events):
    return lax.optimization_barrier((tuple(values), tuple(events)))[0]


def scatter(pieces, axis="x"):
    return [pieces[0]] + [shift(pieces[k], axis, k) for k in (1, 2, 3)]


def body(
    head_values,
    gate_values,
    write_keys,
    read_keys,
    step_size,
    decay_rate,
    skip_weight,
    prior_state,
    norm_gain,
    out_weight,
    residual,
):
    place = jnp.stack([lax.axis_index(name) for name in ("core", "x", "y", "z")]).astype(jnp.int32)
    rate = decay_rate[None, :]

    steps = step_size.T
    from_below, from_above = shift(out_weight, "z", 1), shift(out_weight, "z", -1)
    keep, send = local_state(place, head_values, write_keys, steps, rate)
    got = swap(send)
    chips = chip_total(place, keep, got)
    plain, scale = plain_part(
        head_values, gate_values, write_keys, read_keys, steps, rate, skip_weight[None, :], chips[0]
    )
    prior = turned_prior(place, prior_state, chips[0])
    row, before = row_total(place, scatter(chips, "y"), (plain, prior))
    rows = scatter([row] * 4, "z")
    kept = [out_weight, from_above, from_below]
    swapped = [swap(part) for part in kept]
    entering = scatter(row_enter(place, rows, before, prior, kept[1:]), "y")
    depth = out_weight.shape[0] // 2
    kept += [shift(from_below[:depth], "z", 1), shift(from_above[depth:], "z", -1)]
    mine, other = entering_state(place, entering, keep, got)
    other = swap(other)
    top, low, stats = gated_part(place, mine, other, read_keys, plain, scale, norm_gain[None, :])
    swapped += [swap(part) for part in later(kept[3:], [stats])]
    weights = kept + swapped

    top_below, top_above = shift(top, "y", 1), shift(top, "y", -1)
    low_below, low_above = shift(low, "y", 1), shift(low, "y", -1)

    own = scatter(project(place, top, low, weights, stats))
    first = project(place, top_below, top_above, weights, None, own[:1])
    top_go, low_go = later((top_below, low_above), (top_above, low_below, first[0]))
    top_far, low_far = shift(top_go, "y", 1), shift(low_go, "y", -1)
    second = project(place, low_below, low_above, weights, None, own[1:] + first[:1])
    first = scatter(first)
    far = scatter(project(place, top_far, low_far, weights, None, first[1:] + second[:1]))
    second = scatter(second)

    down, up = neighbour_sums(first, second)
    from_above = shift(down, "y", -1)
    from_below = shift(up, "y", 1)
    from_far = shift(far_sums(far), "y", 2)
    return finish(place, own, from_above, from_far, from_below, residual)


def solution(mesh):
    grid = Mesh(mesh.devices.reshape(4, 4, 2, 4), ("z", "y", "core", "x"))
    ctx = ("z", "y", "core")
    in_specs = (
        P(ctx, "x"),
        P(ctx, "x"),
        P(ctx, None),
        P(ctx, None),
        P(ctx, "x"),
        P("x"),
        P("x"),
        P("x", None, None),
        P("x"),
        P("x", ctx),
        P(ctx, "x"),
    )
    return jax.shard_map(
        body, mesh=grid, in_specs=in_specs, out_specs=P(ctx, "x"), check_vma=False
    )
```

```python
import functools

import jax
import jax.numpy as jnp
from jax import lax
from jax.experimental import pallas as pl
from jax.experimental.pallas import tpu as pltpu
from jax.sharding import Mesh, PartitionSpec as P

EPSILON = 1e-05
ROWS = 256
HALF = 128
HEADS = 16
WIDTH = 128
LANES = HEADS * WIDTH
SLICE = LANES // 8
SPLIT = LANES // 2
PIECE = 512
INNER = 8192
SHARE = 1
F32 = jnp.float32
BF16 = jnp.bfloat16
HIGHEST = lax.Precision.HIGHEST
HBM = pl.BlockSpec(memory_space=pltpu.HBM)
VMEM = pl.BlockSpec(memory_space=pltpu.VMEM)
SMEM = pl.BlockSpec(memory_space=pltpu.SMEM)


def params(mib=16):
    return pltpu.CompilerParams(vmem_limit_bytes=mib * 2**20)


ANY = pl.BlockSpec(memory_space=pl.ANY)


def cost(flops, bytes_accessed, transcendentals=0):
    return pl.CostEstimate(
        flops=flops // SHARE, bytes_accessed=bytes_accessed // SHARE, transcendentals=0
    )


def lower(rows):
    return lax.broadcasted_iota(jnp.int32, (rows, rows), 0) >= lax.broadcasted_iota(
        jnp.int32, (rows, rows), 1
    )


def cumulate(step, rate):
    ones = jnp.where(lower(ROWS), 1.0, 0.0).astype(F32)
    column = jnp.broadcast_to(rate, (8, HEADS)).T[:, 0:1]
    return lax.dot_general(
        -step * column,
        ones,
        (((1,), (1,)), ((), ())),
        precision=HIGHEST,
        preferred_element_type=F32,
    )


def three(row):
    high = row.astype(BF16)
    rest = row - high.astype(F32)
    middle = rest.astype(BF16)
    last = (rest - middle.astype(F32)).astype(BF16)
    return high.astype(F32), middle.astype(F32), last.astype(F32)


def stack_rows(rows, count):
    width = rows[0].shape[1]
    index = lax.broadcasted_iota(jnp.int32, (count, width), 0)
    result = jnp.zeros((count, width), F32)
    for place, row in enumerate(rows):
        result = jnp.where(index == place, row, result)
    return result


def unpack_rows(block):
    block = block.astype(F32)
    return block[0:1] + block[1:2] + block[2:3]


def fetch(sources, targets, sems):
    copies = [
        pltpu.make_async_copy(source, target, sems.at[i])
        for i, (source, target) in enumerate(zip(sources, targets))
    ]
    for copy in copies:
        copy.start()
    for copy in copies:
        copy.wait()
    return targets


def room(sources):
    targets = [pltpu.VMEM(source.shape, source.dtype) for source in sources]
    return targets + [pltpu.SemaphoreType.DMA((len(sources),))]


def state_kernel(place, *refs):
    keep_ref, send_ref, state, logs = refs[4:8]
    value_ref, write_ref, step_ref, rate_ref = fetch(refs[0:4], refs[8:12], refs[12])
    core = place[0]
    step = step_ref[...]
    across = cumulate(step, rate_ref[...])
    to_end = (jnp.exp(across[:, ROWS - 1 : ROWS] - across) * step).T
    last = across.T[ROWS - 1 : ROWS]
    write = write_ref[...].T
    for head in range(HEADS):
        at = slice(head * WIDTH, (head + 1) * WIDTH)
        weighted = (value_ref[:, at].astype(F32) * to_end[:, head : head + 1]).astype(BF16)
        state[:, at] = jnp.dot(write, weighted, preferred_element_type=F32)
        logs[:, at] = jnp.broadcast_to(last[:, head : head + 1], (8, WIDTH))
    mine = pl.ds(pl.multiple_of(core * SPLIT, SPLIT), SPLIT)
    other = pl.ds(pl.multiple_of((1 - core) * SPLIT, SPLIT), SPLIT)
    keep_ref[0:WIDTH, :] = state[:, mine]
    keep_ref[WIDTH:, :] = logs[:, mine]
    send_ref[0:WIDTH, :] = state[:, other]
    send_ref[WIDTH:, :] = logs[:, other]


def whole(shape):
    return pl.BlockSpec(shape, lambda i, place: (0,) * len(shape))


def local_state(place, values, writes, steps, rate):
    shape = (WIDTH + 8, SPLIT)
    sources = (values, writes, steps, rate)
    return pl.pallas_call(
        state_kernel,
        out_shape=[jax.ShapeDtypeStruct(shape, F32)] * 2,
        in_specs=[SMEM] + [HBM] * 4,
        out_specs=[VMEM] * 2,
        scratch_shapes=[pltpu.VMEM((WIDTH, LANES), F32), pltpu.VMEM((8, LANES), F32)]
        + room(sources),
        compiler_params=params(),
        cost_estimate=cost(2 * WIDTH * ROWS * LANES, 3 * 2**20),
        name="local_state",
    )(place, *sources)


def plain_kernel(*refs):
    plain_ref, scale_ref = refs[8:10]
    targets = fetch(refs[0:7], refs[10:17], refs[17])
    value_ref, gate_ref, write_ref, read_ref, step_ref, rate_ref, skip_ref = targets
    step = step_ref[...]
    across = cumulate(step, rate_ref[...])
    cumulative = across.T
    decay = jnp.exp(cumulative)
    scores = lax.dot_general(
        read_ref[...], write_ref[...], (((1,), (1,)), ((), ())), preferred_element_type=F32
    )
    scores = jnp.where(lower(ROWS), scores, 0.0)
    for head in range(HEADS):
        at = slice(head * WIDTH, (head + 1) * WIDTH)
        spread = jnp.minimum(cumulative[:, head : head + 1] - across[head : head + 1, :], 0.0)
        mixing = (jnp.exp(spread) * scores * step[head : head + 1, :]).astype(BF16)
        value = value_ref[:, at]
        within = jnp.dot(mixing, value, preferred_element_type=F32)
        within = within + skip_ref[:, head : head + 1] * value.astype(F32)
        gate = gate_ref[:, at].astype(F32)
        gate = gate / (1.0 + jnp.exp(-gate))
        plain_ref[:, at] = within * gate
        scale_ref[:, at] = decay[:, head : head + 1] * gate


def plain_part(values, gates, writes, reads, steps, rate, skip, after):
    shape = jax.ShapeDtypeStruct((ROWS, LANES), F32)
    sources = (values, gates, writes, reads, steps, rate, skip)
    return pl.pallas_call(
        plain_kernel,
        out_shape=(shape, shape),
        in_specs=[HBM] * 7 + [ANY],
        out_specs=(VMEM, VMEM),
        scratch_shapes=room(sources),
        compiler_params=params(),
        cost_estimate=cost(
            2 * ROWS * ROWS * LANES, 7 * 2**20, HEADS * ROWS * ROWS + ROWS * LANES
        ),
        name="plain_part",
    )(*sources, after)


def turn_kernel(place, prior_ref, _, out_ref):
    out_ref[...] = prior_ref[0].T


def turned_prior(place, prior, after):
    heads = 2
    first = lambda place: 4 * place[0] + place[2]
    return pl.pallas_call(
        turn_kernel,
        grid_spec=pltpu.PrefetchScalarGridSpec(
            num_scalar_prefetch=1,
            grid=(heads,),
            in_specs=[
                pl.BlockSpec((1, WIDTH, WIDTH), lambda i, place: (first(place) * heads + i, 0, 0)),
                ANY,
            ],
            out_specs=pl.BlockSpec((WIDTH, WIDTH), lambda i, place: (0, i)),
        ),
        out_shape=jax.ShapeDtypeStruct((WIDTH, SLICE), F32),
        compiler_params=params(),
        cost_estimate=cost(0, 2**20),
        name="turned_prior",
    )(place, prior, after)


MESSAGE = jax.ShapeDtypeStruct((WIDTH + 16, SLICE), BF16)


def write_message(out_ref, state, log):
    out_ref[0:WIDTH, :] = state.astype(BF16)
    out_ref[WIDTH:, :] = stack_rows(three(log), 16).astype(BF16)


def slice_of(place, k):
    return pl.ds(pl.multiple_of(lax.rem(place[2] + k + 4, 4) * SLICE, SLICE), SLICE)


def chip_kernel(place, keep_ref, got_ref, *refs):
    outs, total, logs = refs[-6:-2], refs[-2], refs[-1]
    first = place[0] == 0
    kept, got = keep_ref[...], got_ref[...]
    state0 = jnp.where(first, kept, got)
    state1 = jnp.where(first, got, kept)
    log1 = state1[WIDTH : WIDTH + 1]
    total[...] = jnp.exp(log1) * state0[0:WIDTH] + state1[0:WIDTH]
    logs[...] = state0[WIDTH:] + state1[WIDTH:]
    for k, out_ref in enumerate(outs):
        at = slice_of(place, k)
        write_message(out_ref, total[:, at], logs[0:1, at])


def chip_total(place, keep, got, after):
    pieces = pl.pallas_call(
        chip_kernel,
        out_shape=[MESSAGE] * 4,
        in_specs=[SMEM] + [VMEM] * 2 + [ANY] * len(after),
        out_specs=[VMEM] * 4,
        scratch_shapes=[pltpu.VMEM((WIDTH, SPLIT), F32), pltpu.VMEM((8, SPLIT), F32)],
        compiler_params=params(),
        cost_estimate=cost(2 * WIDTH * SPLIT, 2**20),
        name="chip_total",
    )(place, keep, got, *after)
    return list(pieces)


def fold(here, parts, before):
    logs = [unpack_rows(part[WIDTH : WIDTH + 16, :]) for part in parts]
    at = [lax.rem(here - k + 4, 4) for k in range(4)]
    total = jnp.zeros((WIDTH, SLICE), F32)
    log = jnp.zeros_like(logs[0])
    for k in range(4):
        after = jnp.zeros_like(log)
        for j in range(4):
            if j != k:
                counts = jnp.logical_and(at[j] > at[k], at[j] < before)
                after = after + jnp.where(counts, logs[j], 0.0)
        weight = jnp.where(at[k] < before, jnp.exp(after), 0.0)
        total = total + weight * parts[k][0:WIDTH, :].astype(F32)
        log = log + jnp.where(at[k] < before, logs[k], 0.0)
    return total, log


def row_kernel(place, p0, p1, p2, p3, *refs):
    parts = (p0, p1, p2, p3)
    out_ref, before_ref = refs[-2:]
    write_message(out_ref, *fold(place[2], parts, 4))
    for k in range(4):
        total, log = fold(place[2], parts, lax.rem(place[2] + k, 4))
        before_ref[k, 0:WIDTH, :] = total
        before_ref[k, WIDTH:, :] = jnp.broadcast_to(log, (8, SLICE))


def row_total(place, parts, after):
    return pl.pallas_call(
        row_kernel,
        out_shape=(MESSAGE, jax.ShapeDtypeStruct((4, WIDTH + 8, SLICE), F32)),
        in_specs=[SMEM] + [VMEM] * 4 + [ANY] * len(after),
        out_specs=(VMEM, VMEM),
        compiler_params=params(),
        cost_estimate=cost(40 * WIDTH * SLICE, 2**20),
        name="row_total",
    )(place, *parts, *after)


def row_enter_kernel(place, p0, p1, p2, p3, before_ref, prior_ref, *refs):
    total, log = fold(place[3], (p0, p1, p2, p3), place[3])
    entering = total + jnp.exp(log) * prior_ref[...]
    for k, out_ref in enumerate(refs[-4:]):
        decay = jnp.exp(before_ref[k, WIDTH : WIDTH + 1, :])
        out_ref[...] = (decay * entering + before_ref[k, 0:WIDTH, :]).astype(BF16)


def row_enter(place, parts, before, prior, after):
    pieces = pl.pallas_call(
        row_enter_kernel,
        out_shape=[jax.ShapeDtypeStruct((WIDTH, SLICE), BF16)] * 4,
        in_specs=[SMEM] + [VMEM] * 6 + [ANY] * len(after),
        out_specs=[VMEM] * 4,
        compiler_params=params(),
        cost_estimate=cost(16 * WIDTH * SLICE, 2**20),
        name="row_enter",
    )(place, *parts, before, prior, *after)
    return list(pieces)


def row_enter_all_kernel(place, p0, p1, p2, p3, before_ref, prior_ref, *refs):
    total, log = fold(place[3], (p0, p1, p2, p3), place[3])
    entering = total + jnp.exp(log) * prior_ref[...]
    for at in range(4):
        before = before_ref[lax.rem(at - place[2] + 4, 4)]
        decay = jnp.exp(before[WIDTH : WIDTH + 1, :])
        refs[-1][at] = (decay * entering + before[0:WIDTH, :]).astype(BF16)


def row_enter_all(place, parts, before, prior, after):
    return pl.pallas_call(
        row_enter_all_kernel,
        out_shape=jax.ShapeDtypeStruct((4, WIDTH, SLICE), BF16),
        in_specs=[SMEM] + [VMEM] * 6 + [ANY] * len(after),
        out_specs=VMEM,
        compiler_params=params(),
        cost_estimate=cost(16 * WIDTH * SLICE, 2**20),
        name="row_enter",
    )(place, *parts, before, prior, *after)


def enter_all_kernel(place, parts_ref, keep_ref, got_ref, *refs):
    mine_ref, other_ref, chip = refs[-3:]
    first = place[0] == 0
    for at in range(4):
        chip[:, at * SLICE : (at + 1) * SLICE] = parts_ref[at].astype(F32)
    entering = chip[...]
    state0 = jnp.where(first, keep_ref[...], got_ref[...])
    second = jnp.exp(state0[WIDTH : WIDTH + 1]) * entering + state0[0:WIDTH]
    mine_ref[...] = jnp.where(first, entering, second).astype(BF16)
    other_ref[...] = jnp.where(first, second, entering).astype(BF16)


def entering_state_all(place, parts, keep, got, after=()):
    shape = jax.ShapeDtypeStruct((WIDTH, SPLIT), BF16)
    return pl.pallas_call(
        enter_all_kernel,
        out_shape=(shape, shape),
        in_specs=[SMEM] + [VMEM] * 3 + [ANY] * len(after),
        out_specs=(VMEM, VMEM),
        scratch_shapes=[pltpu.VMEM((WIDTH, SPLIT), F32)],
        compiler_params=params(),
        cost_estimate=cost(8 * WIDTH * SPLIT, 2 * 2**20),
        name="entering_state",
    )(place, parts, keep, got, *after)


def enter_kernel(place, p0, p1, p2, p3, keep_ref, got_ref, *refs):
    mine_ref, other_ref, chip = refs[-3:]
    first = place[0] == 0
    for k, part in enumerate((p0, p1, p2, p3)):
        chip[:, slice_of(place, -k)] = part[...].astype(F32)
    entering = chip[...]
    state0 = jnp.where(first, keep_ref[...], got_ref[...])
    second = jnp.exp(state0[WIDTH : WIDTH + 1]) * entering + state0[0:WIDTH]
    mine_ref[...] = jnp.where(first, entering, second).astype(BF16)
    other_ref[...] = jnp.where(first, second, entering).astype(BF16)


def entering_state(place, parts, keep, got, after=()):
    shape = jax.ShapeDtypeStruct((WIDTH, SPLIT), BF16)
    return pl.pallas_call(
        enter_kernel,
        out_shape=(shape, shape),
        in_specs=[SMEM] + [VMEM] * 6 + [ANY] * len(after),
        out_specs=(VMEM, VMEM),
        scratch_shapes=[pltpu.VMEM((WIDTH, SPLIT), F32)],
        compiler_params=params(),
        cost_estimate=cost(8 * WIDTH * SPLIT, 2 * 2**20),
        name="entering_state",
    )(place, *parts, keep, got, *after)


def gated_kernel(place, mine_ref, other_ref, read_ref, plain_ref, scale_ref, gain_ref, *refs):
    top_ref, low_ref, stat_ref, acc = refs[-4:]
    step = pl.program_id(0)
    mine = place[0] == step // 2
    entering = jnp.where(mine, mine_ref[...], other_ref[...])
    carried = jnp.dot(read_ref[...], entering, preferred_element_type=F32)
    gated = plain_ref[...] + scale_ref[...] * carried
    result = (gated * gain_ref[...]).astype(BF16)
    top_ref[...] = result[:HALF]
    low_ref[...] = result[HALF:]
    square = gated * gated
    part = square[:, 0:128]
    for at in range(128, square.shape[1], 128):
        part = part + square[:, at : at + 128]

    @pl.when(step == 0)
    def _():
        acc[...] = part

    @pl.when(step > 0)
    def _():
        acc[...] += part

    @pl.when(step == pl.num_programs(0) - 1)
    def _():
        row = jnp.sum(acc[...].T, axis=0, keepdims=True)
        stat_ref[...] = jnp.zeros_like(stat_ref)
        stat_ref[:, 0:ROWS] = stack_rows(three(row), 16).astype(BF16)


def gated_part(place, mine, other, reads, plain, scale, gain, after):
    steps = 4
    width = LANES // steps
    half = pl.BlockSpec((HALF, width), lambda i, place: (0, i))
    wide = pl.BlockSpec((ROWS, width), lambda i, place: (0, i))
    state = pl.BlockSpec((WIDTH, width), lambda i, place: (0, lax.rem(i, 2)))
    return pl.pallas_call(
        gated_kernel,
        grid_spec=pltpu.PrefetchScalarGridSpec(
            num_scalar_prefetch=1,
            grid=(steps,),
            in_specs=[
                state,
                state,
                whole((ROWS, WIDTH)),
                wide,
                wide,
                pl.BlockSpec((1, width), lambda i, place: (0, i)),
            ]
            + [ANY] * len(after),
            out_specs=[half, half, whole((16, PIECE))],
            scratch_shapes=[pltpu.VMEM((ROWS, 128), F32)],
        ),
        out_shape=(
            jax.ShapeDtypeStruct((HALF, LANES), BF16),
            jax.ShapeDtypeStruct((HALF, LANES), BF16),
            jax.ShapeDtypeStruct((16, PIECE), BF16),
        ),
        compiler_params=params(),
        cost_estimate=cost(2 * ROWS * WIDTH * LANES, 6 * 2**20),
        name="gated_part",
    )(place, mine, other, reads, plain, scale, gain, *after)


def multiply(lefts, weights, out):
    depth = LANES // len(weights)
    for row, ref in enumerate(lefts):
        rows = row * HALF
        total = None
        for part, weight in enumerate(weights):
            at = slice(part * depth, (part + 1) * depth)
            term = jnp.dot(ref[:, at], weight[...], preferred_element_type=F32)
            total = term if total is None else total + term
        out[rows : rows + HALF, :] = total.astype(BF16)


def hand_out(place, total, outs):
    core, x, z = place[0], place[1], place[3]
    for k in range(4):
        out_ref = outs[k if k < 3 or len(outs) == 4 else 4]
        j = lax.rem(x + k - z + 4, 4)
        for half in range(2):
            at = slice(half * 256, (half + 1) * 256)
            side = lax.rem(half + core, 2)
            if len(outs) == 5 and k == 2:
                outs[2 + half][...] = total[j, side]
            else:
                out_ref[0 : total.shape[2], at] = total[j, side]


def project_kernel(tall, count, far, stats, ring, place, *refs):
    lefts, refs = refs[:tall], refs[tall:]
    outs, total = refs[-5 - ring : -1], refs[-1]
    for side in range(2):
        own, above, below = refs[side * count : side * count + 3]
        beyond = refs[side * count + 3 : side * count + 3 + far]
        for j, parts in enumerate(((own,), (above,), beyond, (below,))):
            multiply(lefts, parts, total.at[j, side])
    hand_out(place, total, outs)
    for stat in stats:
        for out_ref in outs:
            out_ref[tall * HALF :, :] = refs[stat][...]


def project(place, lefts, weights, stats=None, after=(), ring=False):
    tall = len(lefts)
    rows = tall * HALF + (0 if stats is None else 16)
    extra = () if stats is None else (stats,)
    widths = [PIECE, PIECE, 256, 256, PIECE] if ring else [PIECE] * 4
    count = len(weights) // 2
    place_of_stats = (len(weights),) * len(extra)
    pieces = pl.pallas_call(
        functools.partial(project_kernel, tall, count, count - 3, place_of_stats, int(ring)),
        in_specs=[SMEM] + [VMEM] * (tall + len(weights) + len(extra)) + [ANY] * len(after),
        out_specs=[VMEM] * len(widths),
        out_shape=[jax.ShapeDtypeStruct((rows, width), BF16) for width in widths],
        scratch_shapes=[pltpu.VMEM((4, 2, tall * HALF, 256), BF16)],
        compiler_params=params(24),
        cost_estimate=cost(2 * ROWS * LANES * 4 * PIECE, 10 * 2**20),
        name="project",
    )(place, *lefts, *weights, *extra, *after)
    return list(pieces)


def near_kernel(top_ref, low_ref, *refs):
    out = refs[-1]
    for side in range(2):
        own, above, below = refs[3 * side : 3 * side + 3]
        for j, part in ((0, own), (1, above), (2, below)):
            multiply((top_ref, low_ref), (part,), out.at[j, side])


def project_near(top, low, weights, after):
    return pl.pallas_call(
        near_kernel,
        in_specs=[VMEM] * 8 + [ANY] * len(after),
        out_specs=VMEM,
        out_shape=jax.ShapeDtypeStruct((3, 2, ROWS, 256), BF16),
        compiler_params=params(24),
        cost_estimate=cost(2 * ROWS * LANES * 3 * PIECE, 8 * 2**20),
        name="project_near",
    )(top, low, *weights, *after)


def far_kernel(place, top_ref, low_ref, *refs):
    near, stat_ref, outs, total = refs[-7], refs[-6], refs[-5:-1], refs[-1]
    for j, source in ((0, 0), (1, 1), (3, 2)):
        total[j] = near[source]
    parts = (len(refs) - 7) // 2
    for side in range(2):
        multiply((top_ref, low_ref), refs[parts * side : parts * side + parts], total.at[2, side])
    hand_out(place, total, outs)
    for out_ref in outs:
        out_ref[ROWS:, :] = stat_ref[...]


def project_far(place, top, low, weights, near, stats):
    pieces = pl.pallas_call(
        far_kernel,
        in_specs=[SMEM] + [VMEM] * (4 + len(weights)),
        out_specs=[VMEM] * 4,
        out_shape=[jax.ShapeDtypeStruct((ROWS + 16, PIECE), BF16)] * 4,
        scratch_shapes=[pltpu.VMEM((4, 2, ROWS, 256), BF16)],
        compiler_params=params(24),
        cost_estimate=cost(2 * ROWS * LANES * PIECE, 4 * 2**20),
        name="project_far",
    )(place, top, low, *weights, near, stats)
    return list(pieces)


def add(parts, rows):
    total = parts[0][rows, :].astype(F32)
    for part in parts[1:]:
        total = total + part[rows, :].astype(F32)
    return total


def start_of(part):
    return ROWS if part.shape[0] > 2 * ROWS else 0


def sums_kernel(count, *refs):
    first, second, (down_ref, up_ref) = refs[:count], refs[count:-2], refs[-2:]
    for at, parts in ((0, first), (HALF, second)):
        row = start_of(parts[0])
        down_ref[at : at + HALF, :] = add(parts, slice(row, row + HALF)).astype(BF16)
        up_ref[at : at + HALF, :] = add(parts, slice(row + HALF, row + ROWS)).astype(BF16)


def neighbour_sums(first, second):
    shape = jax.ShapeDtypeStruct((ROWS, PIECE), BF16)
    return pl.pallas_call(
        functools.partial(sums_kernel, len(first)),
        out_shape=(shape, shape),
        in_specs=[VMEM] * (len(first) + len(second)),
        out_specs=(VMEM, VMEM),
        compiler_params=params(),
        cost_estimate=cost(8 * ROWS * PIECE, 10 * ROWS * PIECE * 2),
        name="neighbour_sums",
    )(*first, *second)


def sum_kernel(*refs):
    row = start_of(refs[0])
    refs[-1][...] = add(refs[:-1], slice(row, row + ROWS)).astype(BF16)


def far_sums(parts):
    return pl.pallas_call(
        sum_kernel,
        out_shape=jax.ShapeDtypeStruct((ROWS, PIECE), BF16),
        in_specs=[VMEM] * len(parts),
        out_specs=VMEM,
        compiler_params=params(),
        cost_estimate=cost(4 * ROWS * PIECE, 5 * ROWS * PIECE * 2),
        name="far_sums",
    )(*parts)


def merge_kernel(up_ref, down_ref, left_ref, right_ref, sum_up_ref, sum_down_ref):
    for ref, half_ref, out_ref, at in (
        (up_ref, left_ref, sum_up_ref, 0),
        (down_ref, right_ref, sum_down_ref, 256),
    ):
        out_ref[:, 256 - at : 512 - at] = ref[:, 256 - at : 512 - at]
        total = ref[:, at : at + 256].astype(F32) + half_ref[...].astype(F32)
        out_ref[:, at : at + 256] = total.astype(BF16)


def merge(up, down, left, right):
    shape = jax.ShapeDtypeStruct((ROWS, PIECE), BF16)
    return pl.pallas_call(
        merge_kernel,
        out_shape=(shape, shape),
        in_specs=[VMEM] * 4,
        out_specs=(VMEM, VMEM),
        compiler_params=params(),
        cost_estimate=cost(ROWS * PIECE, 5 * ROWS * PIECE * 2),
        name="merge",
    )(up, down, left, right)


def write_columns(out_ref, residual_ref, scale, total):
    for at in range(0, PIECE, 128):
        cols = slice(at, at + 128)
        out_ref[:, cols] = (residual_ref[:, cols].astype(F32) + scale * total[:, cols]).astype(BF16)


def finish_kernel(tall, place, p0, p1, p2, p3, up_ref, down_ref, residual_ref, _, out_ref, scale_ref):
    own = (p0, p1, p2, p3)
    step = pl.program_id(0)

    @pl.when(step == 0)
    def _():
        square = sum(unpack_rows(part[tall : tall + 16, 0:ROWS]) for part in own)
        row = lax.rsqrt(square / INNER + EPSILON)
        scale_ref[...] = jnp.broadcast_to(row, (128, ROWS)).T
        write_columns(out_ref, residual_ref, scale_ref[...], add(own, slice(0, ROWS)))

    for k, ref in ((1, up_ref), (2, down_ref)):

        @pl.when(step == k)
        def _(ref=ref):
            write_columns(out_ref, residual_ref, scale_ref[...], ref[...].astype(F32))


OUT = jax.ShapeDtypeStruct((ROWS, 4 * PIECE), BF16)


def finish(place, own, up, down, residual, after):
    block = pl.BlockSpec(
        (ROWS, PIECE), lambda i, place: (0, lax.rem(place[2] + jnp.where(i == 2, 3, i), 4))
    )
    return pl.pallas_call(
        functools.partial(finish_kernel, own[0].shape[0] - 16),
        grid_spec=pltpu.PrefetchScalarGridSpec(
            num_scalar_prefetch=1,
            grid=(3,),
            in_specs=[whole(own[0].shape)] * 4 + [whole((ROWS, PIECE))] * 2 + [block, ANY],
            out_specs=[block, whole((ROWS, 128))],
        ),
        out_shape=(OUT, jax.ShapeDtypeStruct((ROWS, 128), F32)),
        compiler_params=params(),
        cost_estimate=cost(4 * ROWS * 3 * PIECE, 3 * 2**20),
        name="finish",
    )(place, *own, up, down, residual, after)


def finish_far_kernel(place, far_ref, scale_ref, residual_ref, _, out_ref):
    write_columns(out_ref, residual_ref, scale_ref[...], far_ref[...].astype(F32))


def finish_far(place, far, scale, residual, out):
    block = pl.BlockSpec((ROWS, PIECE), lambda i, place: (0, lax.rem(place[2] + 2, 4)))
    return pl.pallas_call(
        finish_far_kernel,
        grid_spec=pltpu.PrefetchScalarGridSpec(
            num_scalar_prefetch=1,
            grid=(1,),
            in_specs=[whole((ROWS, PIECE)), whole((ROWS, 128)), block, ANY],
            out_specs=block,
        ),
        out_shape=OUT,
        input_output_aliases={4: 0},
        compiler_params=params(),
        cost_estimate=cost(4 * ROWS * PIECE, 2**20),
        name="finish_far",
    )(place, far, scale, residual, out)


def shift(value, axis, by):
    return lax.ppermute(value, axis, [(i, (i + by) % 4) for i in range(4)])


def swap(value):
    return lax.ppermute(value, "core", [(0, 1), (1, 0)])


def later(values, events):
    return lax.optimization_barrier((tuple(values), tuple(events)))[0]


def scatter(pieces, axis="x"):
    if len(pieces) == 4:
        return [pieces[0]] + [shift(pieces[k], axis, k) for k in (1, 2, 3)]
    here, up, left, right, down = pieces
    up, down = merge(up, down, shift(left, axis, 1), shift(right, axis, -1))
    return [here, shift(up, axis, 1), shift(down, axis, -1)]


def body(
    head_values,
    gate_values,
    write_keys,
    read_keys,
    step_size,
    decay_rate,
    skip_weight,
    prior_state,
    norm_gain,
    out_weight,
    residual,
):
    place = jnp.stack([lax.axis_index(name) for name in ("core", "x", "y", "z")]).astype(jnp.int32)
    rate = decay_rate[None, :]

    steps = step_size.T
    from_below, from_above = shift(out_weight, "z", 1), shift(out_weight, "z", -1)
    keep, send = local_state(place, head_values, write_keys, steps, rate)
    got = swap(send)
    weight = [out_weight, from_above, from_below]
    swapped = [swap(out_weight)]
    chips = chip_total(place, keep, got, [])
    sources = (head_values, gate_values, write_keys, read_keys, steps, rate, skip_weight[None, :])
    plain, scale = plain_part(*sources, chips[0])
    prior = turned_prior(place, prior_state, chips[0])
    row, before = row_total(place, scatter(chips, "y"), (prior, plain,))
    rows = scatter([row] * 4, "z")
    swapped += [swap(part) for part in later(weight[1:], rows[1:])]
    entered = row_enter(place, rows, before, prior, [*weight[1:]])
    depth = out_weight.shape[0] // 2
    halves = (from_below[:depth], from_above[depth:])
    halves = later(halves, entered)
    entering = scatter(entered, "y")
    far_weight = [shift(halves[0], "z", 1), shift(halves[1], "z", -1)]
    mine, other = entering_state(place, entering, keep, got, [*swapped])
    other = swap(other)
    gain = norm_gain[None, :]
    top, low, stats = gated_part(place, mine, other, read_keys, plain, scale, gain, [])
    top_below, top_above = shift(top, "y", 1), shift(top, "y", -1)
    near = project_near(top, low, weight + swapped, [])
    far_swapped = [swap(part) for part in later(far_weight, [near])]
    weights = weight + far_weight + swapped + far_swapped
    own = project_far(place, top, low, far_weight + far_swapped, near, stats)
    low_go = low
    (low_go,) = later([low], [top_below, top_above])
    low_below, low_above = shift(low_go, "y", 1), shift(low_go, "y", -1)
    own = scatter(own)
    first = project(place, [top_below, top_above], weights, None, [], False)
    go = (top_below, low_above)
    top_far, low_far = shift(go[0], "y", 1), shift(go[1], "y", -1)
    first = scatter(first)
    second = project(place, [low_below, low_above], weights, None, own[1:] + first[:1], False)
    second = scatter(second)
    far = project(place, [top_far, low_far], weights, None, second[:1], False)
    far = scatter(far)

    down, up = neighbour_sums(first, second)
    from_above = shift(down, "y", -1)
    from_below = shift(up, "y", 1)
    far = far_sums(far)
    from_far = shift(far, "y", 2)
    out, scale = finish(place, own, from_above, from_below, residual, far)
    return finish_far(place, from_far, scale, residual, out)


def solution(mesh):
    grid = Mesh(mesh.devices.reshape(4, 4, 2, 4), ("z", "y", "core", "x"))
    ctx = ("z", "y", "core")
    in_specs = (
        P(ctx, "x"),
        P(ctx, "x"),
        P(ctx, None),
        P(ctx, None),
        P(ctx, "x"),
        P("x"),
        P("x"),
        P("x", None, None),
        P("x"),
        P("x", ctx),
        P(ctx, "x"),
    )
    return jax.shard_map(
        body, mesh=grid, in_specs=in_specs, out_specs=P(ctx, "x"), check_vma=False
    )
```

```python
import functools

import jax
import jax.numpy as jnp
from jax import lax
from jax.experimental import pallas as pl
from jax.experimental.pallas import tpu as pltpu
from jax.sharding import Mesh, PartitionSpec as P

EPSILON = 1e-05
ROWS = 256
HALF = 128
HEADS = 16
WIDTH = 128
LANES = HEADS * WIDTH
SLICE = LANES // 8
SPLIT = LANES // 2
PIECE = 512
INNER = 8192
SHARE = 1
F32 = jnp.float32
BF16 = jnp.bfloat16
HIGHEST = lax.Precision.HIGHEST
VMEM = pl.BlockSpec(memory_space=pltpu.VMEM)
SMEM = pl.BlockSpec(memory_space=pltpu.SMEM)


def params(mib=16):
    return pltpu.CompilerParams(vmem_limit_bytes=mib * 2**20)


ANY = pl.BlockSpec(memory_space=pl.ANY)


def cost(flops, bytes_accessed, transcendentals=0):
    return pl.CostEstimate(
        flops=flops // SHARE, bytes_accessed=bytes_accessed // SHARE, transcendentals=0
    )


def lower(rows):
    return lax.broadcasted_iota(jnp.int32, (rows, rows), 0) >= lax.broadcasted_iota(
        jnp.int32, (rows, rows), 1
    )


def cumulate(packed):
    ones = jnp.where(lower(ROWS), 1.0, 0.0).astype(F32)
    cumulative = lax.dot_general(
        packed[HEADS:],
        ones,
        (((1,), (1,)), ((), ())),
        precision=HIGHEST,
        preferred_element_type=F32,
    )
    return packed[:HEADS], cumulative


def three(row):
    high = row.astype(BF16)
    rest = row - high.astype(F32)
    middle = rest.astype(BF16)
    last = (rest - middle.astype(F32)).astype(BF16)
    return high.astype(F32), middle.astype(F32), last.astype(F32)


def stack_rows(rows, count):
    width = rows[0].shape[1]
    index = lax.broadcasted_iota(jnp.int32, (count, width), 0)
    result = jnp.zeros((count, width), F32)
    for place, row in enumerate(rows):
        result = jnp.where(index == place, row, result)
    return result


def unpack_rows(block):
    block = block.astype(F32)
    return block[0:1] + block[1:2] + block[2:3]


def state_kernel(place, value_ref, write_ref, packed_ref, keep_ref, send_ref, state, logs):
    core = place[0]
    step, across = cumulate(packed_ref[...])
    to_end = (jnp.exp(across[:, ROWS - 1 : ROWS] - across) * step).T
    last = across.T[ROWS - 1 : ROWS]
    write = write_ref[...].T
    for head in range(HEADS):
        at = slice(head * WIDTH, (head + 1) * WIDTH)
        weighted = (value_ref[:, at].astype(F32) * to_end[:, head : head + 1]).astype(BF16)
        state[:, at] = jnp.dot(write, weighted, preferred_element_type=F32)
        logs[:, at] = jnp.broadcast_to(last[:, head : head + 1], (8, WIDTH))
    mine = pl.ds(pl.multiple_of(core * SPLIT, SPLIT), SPLIT)
    other = pl.ds(pl.multiple_of((1 - core) * SPLIT, SPLIT), SPLIT)
    keep_ref[0:WIDTH, :] = state[:, mine]
    keep_ref[WIDTH:, :] = logs[:, mine]
    send_ref[0:WIDTH, :] = state[:, other]
    send_ref[WIDTH:, :] = logs[:, other]


def whole(shape):
    return pl.BlockSpec(shape, lambda i, place: (0,) * len(shape))


def local_state(place, *sources):
    shape = (WIDTH + 8, SPLIT)
    return pl.pallas_call(
        state_kernel,
        out_shape=[jax.ShapeDtypeStruct(shape, F32)] * 2,
        in_specs=[SMEM] + [VMEM] * 3,
        out_specs=[VMEM] * 2,
        scratch_shapes=[pltpu.VMEM((WIDTH, LANES), F32), pltpu.VMEM((8, LANES), F32)],
        compiler_params=params(),
        cost_estimate=cost(2 * WIDTH * ROWS * LANES, 3 * 2**20),
        name="local_state",
    )(place, *sources)


def plain_kernel(
    value_ref, gate_ref, write_ref, read_ref, packed_ref, skip_ref, _, plain_ref, scale_ref
):
    step, across = cumulate(packed_ref[...])
    cumulative = across.T
    decay = jnp.exp(cumulative)
    scores = lax.dot_general(
        read_ref[...], write_ref[...], (((1,), (1,)), ((), ())), preferred_element_type=F32
    )
    scores = jnp.where(lower(ROWS), scores, 0.0)
    for head in range(HEADS):
        at = slice(head * WIDTH, (head + 1) * WIDTH)
        spread = jnp.minimum(cumulative[:, head : head + 1] - across[head : head + 1, :], 0.0)
        mixing = (jnp.exp(spread) * scores * step[head : head + 1, :]).astype(BF16)
        value = value_ref[:, at]
        within = jnp.dot(mixing, value, preferred_element_type=F32)
        within = within + skip_ref[:, head : head + 1] * value.astype(F32)
        gate = gate_ref[:, at].astype(F32)
        gate = gate / (1.0 + jnp.exp(-gate))
        plain_ref[:, at] = within * gate
        scale_ref[:, at] = decay[:, head : head + 1] * gate


def plain_part(*sources):
    shape = jax.ShapeDtypeStruct((ROWS, LANES), F32)
    return pl.pallas_call(
        plain_kernel,
        out_shape=(shape, shape),
        in_specs=[VMEM] * 6 + [ANY],
        out_specs=(VMEM, VMEM),
        compiler_params=params(),
        cost_estimate=cost(
            2 * ROWS * ROWS * LANES, 7 * 2**20, HEADS * ROWS * ROWS + ROWS * LANES
        ),
        name="plain_part",
    )(*sources)


def turn_kernel(place, prior_ref, _, out_ref):
    out_ref[...] = prior_ref[0].T


def turned_prior(place, prior, after):
    heads = 2
    first = lambda place: 4 * place[0] + place[2]
    return pl.pallas_call(
        turn_kernel,
        grid_spec=pltpu.PrefetchScalarGridSpec(
            num_scalar_prefetch=1,
            grid=(heads,),
            in_specs=[
                pl.BlockSpec((1, WIDTH, WIDTH), lambda i, place: (first(place) * heads + i, 0, 0)),
                ANY,
            ],
            out_specs=pl.BlockSpec((WIDTH, WIDTH), lambda i, place: (0, i)),
        ),
        out_shape=jax.ShapeDtypeStruct((WIDTH, SLICE), F32),
        compiler_params=params(),
        cost_estimate=cost(0, 2**20),
        name="turned_prior",
    )(place, prior, after)


MESSAGE = jax.ShapeDtypeStruct((WIDTH + 16, SLICE), BF16)


def write_message(out_ref, state, log):
    out_ref[0:WIDTH, :] = state.astype(BF16)
    out_ref[WIDTH:, :] = stack_rows(three(log), 16).astype(BF16)


def slice_of(place, k):
    return pl.ds(pl.multiple_of(lax.rem(place[2] + k + 4, 4) * SLICE, SLICE), SLICE)


def chip_kernel(place, keep_ref, got_ref, *refs):
    outs, total, logs = refs[-6:-2], refs[-2], refs[-1]
    first = place[0] == 0
    kept, got = keep_ref[...], got_ref[...]
    state0 = jnp.where(first, kept, got)
    state1 = jnp.where(first, got, kept)
    log1 = state1[WIDTH : WIDTH + 1]
    total[...] = jnp.exp(log1) * state0[0:WIDTH] + state1[0:WIDTH]
    logs[...] = state0[WIDTH:] + state1[WIDTH:]
    for k, out_ref in enumerate(outs):
        at = slice_of(place, k)
        write_message(out_ref, total[:, at], logs[0:1, at])


def chip_total(place, keep, got, after):
    pieces = pl.pallas_call(
        chip_kernel,
        out_shape=[MESSAGE] * 4,
        in_specs=[SMEM] + [VMEM] * 2 + [ANY] * len(after),
        out_specs=[VMEM] * 4,
        scratch_shapes=[pltpu.VMEM((WIDTH, SPLIT), F32), pltpu.VMEM((8, SPLIT), F32)],
        compiler_params=params(),
        cost_estimate=cost(2 * WIDTH * SPLIT, 2**20),
        name="chip_total",
    )(place, keep, got, *after)
    return list(pieces)


def fold(here, parts, before):
    logs = [unpack_rows(part[WIDTH : WIDTH + 16, :]) for part in parts]
    at = [lax.rem(here - k + 4, 4) for k in range(4)]
    total = jnp.zeros((WIDTH, SLICE), F32)
    log = jnp.zeros_like(logs[0])
    for k in range(4):
        after = jnp.zeros_like(log)
        for j in range(4):
            if j != k:
                counts = jnp.logical_and(at[j] > at[k], at[j] < before)
                after = after + jnp.where(counts, logs[j], 0.0)
        weight = jnp.where(at[k] < before, jnp.exp(after), 0.0)
        total = total + weight * parts[k][0:WIDTH, :].astype(F32)
        log = log + jnp.where(at[k] < before, logs[k], 0.0)
    return total, log


def row_kernel(place, p0, p1, p2, p3, *refs):
    parts = (p0, p1, p2, p3)
    out_ref, before_ref = refs[-2:]
    write_message(out_ref, *fold(place[2], parts, 4))
    for k in range(4):
        total, log = fold(place[2], parts, lax.rem(place[2] + k, 4))
        before_ref[k, 0:WIDTH, :] = total
        before_ref[k, WIDTH:, :] = jnp.broadcast_to(log, (8, SLICE))


def row_total(place, parts, after):
    return pl.pallas_call(
        row_kernel,
        out_shape=(MESSAGE, jax.ShapeDtypeStruct((4, WIDTH + 8, SLICE), F32)),
        in_specs=[SMEM] + [VMEM] * 4 + [ANY] * len(after),
        out_specs=(VMEM, VMEM),
        compiler_params=params(),
        cost_estimate=cost(40 * WIDTH * SLICE, 2**20),
        name="row_total",
    )(place, *parts, *after)


def row_enter_kernel(place, p0, p1, p2, p3, before_ref, prior_ref, *refs):
    total, log = fold(place[3], (p0, p1, p2, p3), place[3])
    entering = total + jnp.exp(log) * prior_ref[...]
    for k, out_ref in enumerate(refs[-4:]):
        decay = jnp.exp(before_ref[k, WIDTH : WIDTH + 1, :])
        out_ref[...] = (decay * entering + before_ref[k, 0:WIDTH, :]).astype(BF16)


def row_enter(place, parts, before, prior, after):
    pieces = pl.pallas_call(
        row_enter_kernel,
        out_shape=[jax.ShapeDtypeStruct((WIDTH, SLICE), BF16)] * 4,
        in_specs=[SMEM] + [VMEM] * 6 + [ANY] * len(after),
        out_specs=[VMEM] * 4,
        compiler_params=params(),
        cost_estimate=cost(16 * WIDTH * SLICE, 2**20),
        name="row_enter",
    )(place, *parts, before, prior, *after)
    return list(pieces)


def row_enter_all_kernel(place, p0, p1, p2, p3, before_ref, prior_ref, *refs):
    total, log = fold(place[3], (p0, p1, p2, p3), place[3])
    entering = total + jnp.exp(log) * prior_ref[...]
    for at in range(4):
        before = before_ref[lax.rem(at - place[2] + 4, 4)]
        decay = jnp.exp(before[WIDTH : WIDTH + 1, :])
        refs[-1][at] = (decay * entering + before[0:WIDTH, :]).astype(BF16)


def row_enter_all(place, parts, before, prior, after):
    return pl.pallas_call(
        row_enter_all_kernel,
        out_shape=jax.ShapeDtypeStruct((4, WIDTH, SLICE), BF16),
        in_specs=[SMEM] + [VMEM] * 6 + [ANY] * len(after),
        out_specs=VMEM,
        compiler_params=params(),
        cost_estimate=cost(16 * WIDTH * SLICE, 2**20),
        name="row_enter",
    )(place, *parts, before, prior, *after)


def enter_all_kernel(place, parts_ref, keep_ref, got_ref, *refs):
    mine_ref, other_ref, chip = refs[-3:]
    first = place[0] == 0
    for at in range(4):
        chip[:, at * SLICE : (at + 1) * SLICE] = parts_ref[at].astype(F32)
    entering = chip[...]
    state0 = jnp.where(first, keep_ref[...], got_ref[...])
    second = jnp.exp(state0[WIDTH : WIDTH + 1]) * entering + state0[0:WIDTH]
    mine_ref[...] = jnp.where(first, entering, second).astype(BF16)
    other_ref[...] = jnp.where(first, second, entering).astype(BF16)


def entering_state_all(place, parts, keep, got, after=()):
    shape = jax.ShapeDtypeStruct((WIDTH, SPLIT), BF16)
    return pl.pallas_call(
        enter_all_kernel,
        out_shape=(shape, shape),
        in_specs=[SMEM] + [VMEM] * 3 + [ANY] * len(after),
        out_specs=(VMEM, VMEM),
        scratch_shapes=[pltpu.VMEM((WIDTH, SPLIT), F32)],
        compiler_params=params(),
        cost_estimate=cost(8 * WIDTH * SPLIT, 2 * 2**20),
        name="entering_state",
    )(place, parts, keep, got, *after)


def enter_kernel(place, p0, p1, p2, p3, keep_ref, got_ref, *refs):
    mine_ref, other_ref, chip = refs[-3:]
    first = place[0] == 0
    for k, part in enumerate((p0, p1, p2, p3)):
        chip[:, slice_of(place, -k)] = part[...].astype(F32)
    entering = chip[...]
    state0 = jnp.where(first, keep_ref[...], got_ref[...])
    second = jnp.exp(state0[WIDTH : WIDTH + 1]) * entering + state0[0:WIDTH]
    mine_ref[...] = jnp.where(first, entering, second).astype(BF16)
    other_ref[...] = jnp.where(first, second, entering).astype(BF16)


def entering_state(place, parts, keep, got, after=()):
    shape = jax.ShapeDtypeStruct((WIDTH, SPLIT), BF16)
    return pl.pallas_call(
        enter_kernel,
        out_shape=(shape, shape),
        in_specs=[SMEM] + [VMEM] * 6 + [ANY] * len(after),
        out_specs=(VMEM, VMEM),
        scratch_shapes=[pltpu.VMEM((WIDTH, SPLIT), F32)],
        compiler_params=params(),
        cost_estimate=cost(8 * WIDTH * SPLIT, 2 * 2**20),
        name="entering_state",
    )(place, *parts, keep, got, *after)


def gated_kernel(place, mine_ref, other_ref, read_ref, plain_ref, scale_ref, gain_ref, *refs):
    top_ref, low_ref, stat_ref = refs[-3:]
    read = read_ref[...]
    width = 256
    part = None
    for start in range(0, LANES, width):
        at = slice(start, start + width)
        source = slice(start % SPLIT, start % SPLIT + width)
        mine = place[0] == start // SPLIT
        entering = jnp.where(mine, mine_ref[:, source], other_ref[:, source])
        carried = jnp.dot(read, entering, preferred_element_type=F32)
        gated = plain_ref[:, at] + scale_ref[:, at] * carried
        result = (gated * gain_ref[:, at]).astype(BF16)
        top_ref[:, at] = result[:HALF]
        low_ref[:, at] = result[HALF:]
        square = gated * gated
        square = square[:, :128] + square[:, 128:]
        part = square if part is None else part + square
    row = jnp.sum(part.T, axis=0, keepdims=True)
    stat_ref[...] = jnp.zeros_like(stat_ref)
    stat_ref[:, 0:ROWS] = stack_rows(three(row), 16).astype(BF16)


def gated_part(place, mine, other, reads, plain, scale, gain, after):
    return pl.pallas_call(
        gated_kernel,
        out_shape=(
            jax.ShapeDtypeStruct((HALF, LANES), BF16),
            jax.ShapeDtypeStruct((HALF, LANES), BF16),
            jax.ShapeDtypeStruct((16, PIECE), BF16),
        ),
        in_specs=[SMEM] + [VMEM] * 6 + [ANY] * len(after),
        out_specs=[VMEM] * 3,
        compiler_params=params(),
        cost_estimate=cost(2 * ROWS * WIDTH * LANES, 6 * 2**20),
        name="gated_part",
    )(place, mine, other, reads, plain, scale, gain, *after)


def multiply(lefts, weights, out):
    depth = LANES // len(weights)
    for row, ref in enumerate(lefts):
        rows = row * HALF
        total = None
        for part, weight in enumerate(weights):
            at = slice(part * depth, (part + 1) * depth)
            term = jnp.dot(ref[:, at], weight[...], preferred_element_type=F32)
            total = term if total is None else total + term
        out[rows : rows + HALF, :] = total.astype(BF16)


def hand_out(place, total, outs):
    core, x, z = place[0], place[1], place[3]
    for k in range(4):
        out_ref = outs[k if k < 3 or len(outs) == 4 else 4]
        j = lax.rem(x + k - z + 4, 4)
        for half in range(2):
            at = slice(half * 256, (half + 1) * 256)
            side = lax.rem(half + core, 2)
            if len(outs) == 5 and k == 2:
                outs[2 + half][...] = total[j, side]
            else:
                out_ref[0 : total.shape[2], at] = total[j, side]


def project_kernel(tall, count, far, stats, ring, place, *refs):
    lefts, refs = refs[:tall], refs[tall:]
    outs, total = refs[-5 - ring : -1], refs[-1]
    for side in range(2):
        own, above, below = refs[side * count : side * count + 3]
        beyond = refs[side * count + 3 : side * count + 3 + far]
        for j, parts in enumerate(((own,), (above,), beyond, (below,))):
            multiply(lefts, parts, total.at[j, side])
    hand_out(place, total, outs)
    for stat in stats:
        for out_ref in outs:
            out_ref[tall * HALF :, :] = refs[stat][...]


def project(place, lefts, weights, stats=None, after=(), ring=False):
    tall = len(lefts)
    rows = tall * HALF + (0 if stats is None else 16)
    extra = () if stats is None else (stats,)
    widths = [PIECE, PIECE, 256, 256, PIECE] if ring else [PIECE] * 4
    count = len(weights) // 2
    place_of_stats = (len(weights),) * len(extra)
    pieces = pl.pallas_call(
        functools.partial(project_kernel, tall, count, count - 3, place_of_stats, int(ring)),
        in_specs=[SMEM] + [VMEM] * (tall + len(weights) + len(extra)) + [ANY] * len(after),
        out_specs=[VMEM] * len(widths),
        out_shape=[jax.ShapeDtypeStruct((rows, width), BF16) for width in widths],
        scratch_shapes=[pltpu.VMEM((4, 2, tall * HALF, 256), BF16)],
        compiler_params=params(24),
        cost_estimate=cost(2 * ROWS * LANES * 4 * PIECE, 10 * 2**20),
        name="project",
    )(place, *lefts, *weights, *extra, *after)
    return list(pieces)


def hold_kernel(value_ref, out_ref):
    out_ref[...] = value_ref[...]


def hold(value, micros):
    return pl.pallas_call(
        hold_kernel,
        out_shape=jax.ShapeDtypeStruct(value.shape, value.dtype),
        in_specs=[VMEM],
        out_specs=VMEM,
        compiler_params=params(),
        cost_estimate=pl.CostEstimate(
            flops=micros * 10**9, bytes_accessed=2**20, transcendentals=0
        ),
        name="hold",
    )(value)


def near_kernel(top_ref, low_ref, *refs):
    out = refs[-1]
    for side in range(2):
        own, above, below = refs[3 * side : 3 * side + 3]
        for j, part in ((0, own), (1, above), (2, below)):
            multiply((top_ref, low_ref), (part,), out.at[j, side])


def project_near(top, low, weights, after):
    return pl.pallas_call(
        near_kernel,
        in_specs=[VMEM] * 8 + [ANY] * len(after),
        out_specs=VMEM,
        out_shape=jax.ShapeDtypeStruct((3, 2, ROWS, 256), BF16),
        compiler_params=params(24),
        cost_estimate=cost(2 * ROWS * LANES * 3 * PIECE, 2 * 4 * 2**20),
        name="project_near",
    )(top, low, *weights, *after)


def far_kernel(place, top_ref, low_ref, *refs):
    near, stat_ref, outs, total = refs[-7], refs[-6], refs[-5:-1], refs[-1]
    for j, source in ((0, 0), (1, 1), (3, 2)):
        total[j] = near[source]
    parts = (len(refs) - 7) // 2
    for side in range(2):
        multiply((top_ref, low_ref), refs[parts * side : parts * side + parts], total.at[2, side])
    hand_out(place, total, outs)
    for out_ref in outs:
        out_ref[ROWS:, :] = stat_ref[...]


def project_far(place, top, low, weights, near, stats):
    pieces = pl.pallas_call(
        far_kernel,
        in_specs=[SMEM] + [VMEM] * (4 + len(weights)),
        out_specs=[VMEM] * 4,
        out_shape=[jax.ShapeDtypeStruct((ROWS + 16, PIECE), BF16)] * 4,
        scratch_shapes=[pltpu.VMEM((4, 2, ROWS, 256), BF16)],
        compiler_params=params(24),
        cost_estimate=cost(2 * ROWS * LANES * PIECE, 2 * 2 * 2**20),
        name="project_far",
    )(place, top, low, *weights, near, stats)
    return list(pieces)


def add(parts, rows):
    total = parts[0][rows, :].astype(F32)
    for part in parts[1:]:
        total = total + part[rows, :].astype(F32)
    return total


def start_of(part):
    return ROWS if part.shape[0] > 2 * ROWS else 0


def sums_kernel(count, *refs):
    first, second, (down_ref, up_ref) = refs[:count], refs[count:-2], refs[-2:]
    for at, parts in ((0, first), (HALF, second)):
        row = start_of(parts[0])
        down_ref[at : at + HALF, :] = add(parts, slice(row, row + HALF)).astype(BF16)
        up_ref[at : at + HALF, :] = add(parts, slice(row + HALF, row + ROWS)).astype(BF16)


def neighbour_sums(first, second):
    shape = jax.ShapeDtypeStruct((ROWS, PIECE), BF16)
    return pl.pallas_call(
        functools.partial(sums_kernel, len(first)),
        out_shape=(shape, shape),
        in_specs=[VMEM] * (len(first) + len(second)),
        out_specs=(VMEM, VMEM),
        compiler_params=params(),
        cost_estimate=cost(8 * ROWS * PIECE, 10 * ROWS * PIECE * 2),
        name="neighbour_sums",
    )(*first, *second)


def sum_kernel(*refs):
    row = start_of(refs[0])
    refs[-1][...] = add(refs[:-1], slice(row, row + ROWS)).astype(BF16)


def far_sums(parts):
    return pl.pallas_call(
        sum_kernel,
        out_shape=jax.ShapeDtypeStruct((ROWS, PIECE), BF16),
        in_specs=[VMEM] * len(parts),
        out_specs=VMEM,
        compiler_params=params(),
        cost_estimate=cost(4 * ROWS * PIECE, 5 * ROWS * PIECE * 2),
        name="far_sums",
    )(*parts)


def merge_kernel(up_ref, down_ref, left_ref, right_ref, sum_up_ref, sum_down_ref):
    for ref, half_ref, out_ref, at in (
        (up_ref, left_ref, sum_up_ref, 0),
        (down_ref, right_ref, sum_down_ref, 256),
    ):
        out_ref[:, 256 - at : 512 - at] = ref[:, 256 - at : 512 - at]
        total = ref[:, at : at + 256].astype(F32) + half_ref[...].astype(F32)
        out_ref[:, at : at + 256] = total.astype(BF16)


def merge(up, down, left, right):
    shape = jax.ShapeDtypeStruct((ROWS, PIECE), BF16)
    return pl.pallas_call(
        merge_kernel,
        out_shape=(shape, shape),
        in_specs=[VMEM] * 4,
        out_specs=(VMEM, VMEM),
        compiler_params=params(),
        cost_estimate=cost(ROWS * PIECE, 5 * ROWS * PIECE * 2),
        name="merge",
    )(up, down, left, right)


def write_columns(out_ref, residual_ref, scale, total):
    for at in range(0, PIECE, 128):
        cols = slice(at, at + 128)
        out_ref[:, cols] = (residual_ref[:, cols].astype(F32) + scale * total[:, cols]).astype(BF16)


def finish_kernel(tall, place, p0, p1, p2, p3, up_ref, down_ref, residual_ref, _, out_ref, scale_ref):
    own = (p0, p1, p2, p3)
    step = pl.program_id(0)

    @pl.when(step == 0)
    def _():
        square = sum(unpack_rows(part[tall : tall + 16, 0:ROWS]) for part in own)
        row = lax.rsqrt(square / INNER + EPSILON)
        scale_ref[...] = jnp.broadcast_to(row, (128, ROWS)).T
        write_columns(out_ref, residual_ref, scale_ref[...], add(own, slice(0, ROWS)))

    for k, ref in ((1, up_ref), (2, down_ref)):

        @pl.when(step == k)
        def _(ref=ref):
            write_columns(out_ref, residual_ref, scale_ref[...], ref[...].astype(F32))


OUT = jax.ShapeDtypeStruct((ROWS, 4 * PIECE), BF16)


def finish(place, own, up, down, residual, after):
    block = pl.BlockSpec(
        (ROWS, PIECE), lambda i, place: (0, lax.rem(place[2] + jnp.where(i == 2, 3, i), 4))
    )
    return pl.pallas_call(
        functools.partial(finish_kernel, own[0].shape[0] - 16),
        grid_spec=pltpu.PrefetchScalarGridSpec(
            num_scalar_prefetch=1,
            grid=(3,),
            in_specs=[whole(own[0].shape)] * 4 + [whole((ROWS, PIECE))] * 2 + [block, ANY],
            out_specs=[block, whole((ROWS, 128))],
        ),
        out_shape=(OUT, jax.ShapeDtypeStruct((ROWS, 128), F32)),
        compiler_params=params(),
        cost_estimate=cost(4 * ROWS * 3 * PIECE, 3 * 2**20),
        name="finish",
    )(place, *own, up, down, residual, after)


def finish_far_kernel(place, far_ref, scale_ref, residual_ref, _, out_ref):
    write_columns(out_ref, residual_ref, scale_ref[...], far_ref[...].astype(F32))


def finish_far(place, far, scale, residual, out):
    block = pl.BlockSpec((ROWS, PIECE), lambda i, place: (0, lax.rem(place[2] + 2, 4)))
    return pl.pallas_call(
        finish_far_kernel,
        grid_spec=pltpu.PrefetchScalarGridSpec(
            num_scalar_prefetch=1,
            grid=(1,),
            in_specs=[whole((ROWS, PIECE)), whole((ROWS, 128)), block, ANY],
            out_specs=block,
        ),
        out_shape=OUT,
        input_output_aliases={4: 0},
        compiler_params=params(),
        cost_estimate=cost(4 * ROWS * PIECE, 2**20),
        name="finish_far",
    )(place, far, scale, residual, out)


def shift(value, axis, by):
    return lax.ppermute(value, axis, [(i, (i + by) % 4) for i in range(4)])


def swap(value):
    return lax.ppermute(value, "core", [(0, 1), (1, 0)])


def later(values, events):
    return lax.optimization_barrier((tuple(values), tuple(events)))[0]


def scatter(pieces, axis="x"):
    if len(pieces) == 4:
        return [pieces[0]] + [shift(pieces[k], axis, k) for k in (1, 2, 3)]
    here, up, left, right, down = pieces
    up, down = merge(up, down, shift(left, axis, 1), shift(right, axis, -1))
    return [here, shift(up, axis, 1), shift(down, axis, -1)]


def body(
    head_values,
    gate_values,
    write_keys,
    read_keys,
    step_size,
    decay_rate,
    skip_weight,
    prior_state,
    norm_gain,
    out_weight,
    residual,
):
    place = jnp.stack([lax.axis_index(name) for name in ("core", "x", "y", "z")]).astype(jnp.int32)

    steps = step_size.T
    packed = jnp.concatenate([steps, -steps * decay_rate[:, None]], axis=0)
    from_below, from_above = shift(out_weight, "z", 1), shift(out_weight, "z", -1)
    keep, send = local_state(place, head_values, write_keys, packed)
    got = swap(send)
    weight = [out_weight, from_above, from_below]
    swapped = [swap(out_weight)]
    chips = chip_total(place, keep, got, [])
    sources = (head_values, gate_values, write_keys, read_keys, packed, skip_weight[None, :])
    plain, scale = plain_part(*sources, chips[0])
    prior = turned_prior(place, prior_state, chips[0])
    row, before = row_total(place, scatter(chips, "y"), (prior, plain,))
    rows = scatter([row] * 4, "z")
    swapped += [swap(part) for part in later(weight[1:], rows[1:])]
    entered = row_enter(place, rows, before, prior, [*weight[1:]])
    depth = out_weight.shape[0] // 2
    halves = (from_below[:depth], from_above[depth:])
    halves = later(halves, entered)
    entering = scatter(entered, "y")
    far_weight = [shift(halves[0], "z", 1), shift(halves[1], "z", -1)]
    mine, other = entering_state(place, entering, keep, got, [*swapped])
    other = swap(other)
    gain = norm_gain[None, :]
    top, low, stats = gated_part(place, mine, other, read_keys, plain, scale, gain, [])
    top_go = top
    top_below, top_above = shift(top_go, "y", 1), shift(top_go, "y", -1)
    near = project_near(top, low, weight + swapped, [])
    far_swapped = [swap(part) for part in later(far_weight, [near])]
    weights = weight + far_weight + swapped + far_swapped
    own = project_far(place, top, low, far_weight + far_swapped, near, stats)
    low_go = low
    (low_go,) = later([low], [top_below, top_above])
    low_below, low_above = shift(low_go, "y", 1), shift(low_go, "y", -1)
    own = scatter(own)
    first = project(place, [top_below, top_above], weights, None, [], False)
    go = (top_below, low_above)
    go = later(go, (top_above, low_below, first[0]))
    top_far, low_far = shift(go[0], "y", 1), shift(go[1], "y", -1)
    first = scatter(first)
    second = project(place, [low_below, low_above], weights, None, own[1:] + first[:1], False)
    second = scatter(second)
    far = project(place, [top_far, low_far], weights, None, second[:1], False)
    far = scatter(far)

    down, up = neighbour_sums(first, second)
    from_above = shift(down, "y", -1)
    from_below = shift(up, "y", 1)
    far = far_sums(far)
    from_far = shift(far, "y", 2)
    out, scale = finish(place, own, from_above, from_below, residual, far)
    return finish_far(place, from_far, scale, residual, out)


def solution(mesh):
    grid = Mesh(mesh.devices.reshape(4, 4, 2, 4), ("z", "y", "core", "x"))
    ctx = ("z", "y", "core")
    in_specs = (
        P(ctx, "x"),
        P(ctx, "x"),
        P(ctx, None),
        P(ctx, None),
        P(ctx, "x"),
        P("x"),
        P("x"),
        P("x", None, None),
        P("x"),
        P("x", ctx),
        P(ctx, "x"),
    )
    return jax.shard_map(
        body, mesh=grid, in_specs=in_specs, out_specs=P(ctx, "x"), check_vma=False
    )
```

```python
import functools

import jax
import jax.numpy as jnp
from jax import lax
from jax.experimental import pallas as pl
from jax.experimental.pallas import tpu as pltpu
from jax.sharding import Mesh, PartitionSpec as P

EPSILON = 1e-05
ROWS = 256
HALF = 128
HEADS = 16
WIDTH = 128
LANES = HEADS * WIDTH
SLICE = LANES // 8
SPLIT = LANES // 2
PIECE = 512
INNER = 8192
SHARE = 1
F32 = jnp.float32
BF16 = jnp.bfloat16
HIGHEST = lax.Precision.HIGHEST
VMEM = pl.BlockSpec(memory_space=pltpu.VMEM)
SMEM = pl.BlockSpec(memory_space=pltpu.SMEM)


def params(mib=16):
    return pltpu.CompilerParams(vmem_limit_bytes=mib * 2**20)


ANY = pl.BlockSpec(memory_space=pl.ANY)


def cost(flops, bytes_accessed, transcendentals=0):
    return pl.CostEstimate(
        flops=flops // SHARE, bytes_accessed=bytes_accessed // SHARE, transcendentals=0
    )


def lower(rows):
    return lax.broadcasted_iota(jnp.int32, (rows, rows), 0) >= lax.broadcasted_iota(
        jnp.int32, (rows, rows), 1
    )


def cumulate(packed):
    ones = jnp.where(lower(ROWS), 1.0, 0.0).astype(F32)
    cumulative = lax.dot_general(
        packed[HEADS:],
        ones,
        (((1,), (1,)), ((), ())),
        precision=HIGHEST,
        preferred_element_type=F32,
    )
    return packed[:HEADS], cumulative


def three(row):
    high = row.astype(BF16)
    rest = row - high.astype(F32)
    middle = rest.astype(BF16)
    last = (rest - middle.astype(F32)).astype(BF16)
    return high.astype(F32), middle.astype(F32), last.astype(F32)


def stack_rows(rows, count):
    width = rows[0].shape[1]
    index = lax.broadcasted_iota(jnp.int32, (count, width), 0)
    result = jnp.zeros((count, width), F32)
    for place, row in enumerate(rows):
        result = jnp.where(index == place, row, result)
    return result


def unpack_rows(block):
    block = block.astype(F32)
    return block[0:1] + block[1:2] + block[2:3]


def state_kernel(place, value_ref, write_ref, packed_ref, keep_ref, send_ref):
    core = place[0]
    step, across = cumulate(packed_ref[...])
    to_end = jnp.exp(across[:, ROWS - 1 : ROWS] - across) * step
    half = HEADS // 2
    turned = lambda rows: jnp.where(
        core == 0, rows, jnp.concatenate([rows[half:], rows[:half]], axis=0)
    )
    to_end = turned(to_end).T
    last = turned(across).T[ROWS - 1 : ROWS]
    write = write_ref[...].T
    for head in range(HEADS):
        from_head = lax.rem(core * half + head, HEADS)
        source = pl.ds(pl.multiple_of(from_head * WIDTH, WIDTH), WIDTH)
        weighted = (value_ref[:, source].astype(F32) * to_end[:, head : head + 1]).astype(BF16)
        out_ref = keep_ref if head < half else send_ref
        at = slice(head % half * WIDTH, (head % half + 1) * WIDTH)
        out_ref[0:WIDTH, at] = jnp.dot(write, weighted, preferred_element_type=F32)
        out_ref[WIDTH:, at] = jnp.broadcast_to(last[:, head : head + 1], (8, WIDTH))


def whole(shape):
    return pl.BlockSpec(shape, lambda i, place: (0,) * len(shape))


def local_state(place, *sources):
    shape = (WIDTH + 8, SPLIT)
    return pl.pallas_call(
        state_kernel,
        out_shape=[jax.ShapeDtypeStruct(shape, F32)] * 2,
        in_specs=[SMEM] + [VMEM] * 3,
        out_specs=[VMEM] * 2,
        compiler_params=params(),
        cost_estimate=cost(2 * WIDTH * ROWS * LANES, 3 * 2**20),
        name="local_state",
    )(place, *sources)


def plain_kernel(
    value_ref, gate_ref, write_ref, read_ref, packed_ref, skip_ref, _, plain_ref, scale_ref
):
    step, across = cumulate(packed_ref[...])
    cumulative = across.T
    decay = jnp.exp(cumulative)
    scores = lax.dot_general(
        read_ref[...], write_ref[...], (((1,), (1,)), ((), ())), preferred_element_type=F32
    )
    scores = jnp.where(lower(ROWS), scores, 0.0)
    for head in range(HEADS):
        at = slice(head * WIDTH, (head + 1) * WIDTH)
        spread = jnp.minimum(cumulative[:, head : head + 1] - across[head : head + 1, :], 0.0)
        mixing = (jnp.exp(spread) * scores * step[head : head + 1, :]).astype(BF16)
        value = value_ref[:, at]
        within = jnp.dot(mixing, value, preferred_element_type=F32)
        within = within + skip_ref[:, head : head + 1] * value.astype(F32)
        gate = gate_ref[:, at].astype(F32)
        gate = gate / (1.0 + jnp.exp(-gate))
        plain_ref[:, at] = within * gate
        scale_ref[:, at] = decay[:, head : head + 1] * gate


def plain_part(*sources):
    shape = jax.ShapeDtypeStruct((ROWS, LANES), F32)
    return pl.pallas_call(
        plain_kernel,
        out_shape=(shape, shape),
        in_specs=[VMEM] * 6 + [ANY],
        out_specs=(VMEM, VMEM),
        compiler_params=params(),
        cost_estimate=cost(
            2 * ROWS * ROWS * LANES, 7 * 2**20, HEADS * ROWS * ROWS + ROWS * LANES
        ),
        name="plain_part",
    )(*sources)


def turn_kernel(place, prior_ref, _, out_ref):
    out_ref[...] = prior_ref[0].T


def turned_prior(place, prior, after):
    heads = 2
    first = lambda place: 4 * place[0] + place[2]
    return pl.pallas_call(
        turn_kernel,
        grid_spec=pltpu.PrefetchScalarGridSpec(
            num_scalar_prefetch=1,
            grid=(heads,),
            in_specs=[
                pl.BlockSpec((1, WIDTH, WIDTH), lambda i, place: (first(place) * heads + i, 0, 0)),
                ANY,
            ],
            out_specs=pl.BlockSpec((WIDTH, WIDTH), lambda i, place: (0, i)),
        ),
        out_shape=jax.ShapeDtypeStruct((WIDTH, SLICE), F32),
        compiler_params=params(),
        cost_estimate=cost(0, 2**20),
        name="turned_prior",
    )(place, prior, after)


MESSAGE = jax.ShapeDtypeStruct((WIDTH + 16, SLICE), BF16)


def write_message(out_ref, state, log):
    out_ref[0:WIDTH, :] = state.astype(BF16)
    out_ref[WIDTH:, :] = stack_rows(three(log), 16).astype(BF16)


def slice_of(place, k):
    return pl.ds(pl.multiple_of(lax.rem(place[2] + k + 4, 4) * SLICE, SLICE), SLICE)


def chip_kernel(place, keep_ref, got_ref, *refs):
    outs, total, logs = refs[-6:-2], refs[-2], refs[-1]
    first = place[0] == 0
    kept, got = keep_ref[...], got_ref[...]
    state0 = jnp.where(first, kept, got)
    state1 = jnp.where(first, got, kept)
    log1 = state1[WIDTH : WIDTH + 1]
    total[...] = jnp.exp(log1) * state0[0:WIDTH] + state1[0:WIDTH]
    logs[...] = state0[WIDTH:] + state1[WIDTH:]
    for k, out_ref in enumerate(outs):
        at = slice_of(place, k)
        write_message(out_ref, total[:, at], logs[0:1, at])


def chip_total(place, keep, got, after):
    pieces = pl.pallas_call(
        chip_kernel,
        out_shape=[MESSAGE] * 4,
        in_specs=[SMEM] + [VMEM] * 2 + [ANY] * len(after),
        out_specs=[VMEM] * 4,
        scratch_shapes=[pltpu.VMEM((WIDTH, SPLIT), F32), pltpu.VMEM((8, SPLIT), F32)],
        compiler_params=params(),
        cost_estimate=cost(2 * WIDTH * SPLIT, 2**20),
        name="chip_total",
    )(place, keep, got, *after)
    return list(pieces)


def fold(here, parts, before):
    logs = [unpack_rows(part[WIDTH : WIDTH + 16, :]) for part in parts]
    at = [lax.rem(here - k + 4, 4) for k in range(4)]
    total = jnp.zeros((WIDTH, SLICE), F32)
    log = jnp.zeros_like(logs[0])
    for k in range(4):
        after = jnp.zeros_like(log)
        for j in range(4):
            if j != k:
                counts = jnp.logical_and(at[j] > at[k], at[j] < before)
                after = after + jnp.where(counts, logs[j], 0.0)
        weight = jnp.where(at[k] < before, jnp.exp(after), 0.0)
        total = total + weight * parts[k][0:WIDTH, :].astype(F32)
        log = log + jnp.where(at[k] < before, logs[k], 0.0)
    return total, log


def row_kernel(place, p0, p1, p2, p3, *refs):
    parts = (p0, p1, p2, p3)
    out_ref, before_ref = refs[-2:]
    write_message(out_ref, *fold(place[2], parts, 4))
    for k in range(4):
        total, log = fold(place[2], parts, lax.rem(place[2] + k, 4))
        before_ref[k, 0:WIDTH, :] = total
        before_ref[k, WIDTH:, :] = jnp.broadcast_to(log, (8, SLICE))


def row_total(place, parts, after):
    return pl.pallas_call(
        row_kernel,
        out_shape=(MESSAGE, jax.ShapeDtypeStruct((4, WIDTH + 8, SLICE), F32)),
        in_specs=[SMEM] + [VMEM] * 4 + [ANY] * len(after),
        out_specs=(VMEM, VMEM),
        compiler_params=params(),
        cost_estimate=cost(40 * WIDTH * SLICE, 2**20),
        name="row_total",
    )(place, *parts, *after)


def row_enter_kernel(place, p0, p1, p2, p3, before_ref, prior_ref, *refs):
    total, log = fold(place[3], (p0, p1, p2, p3), place[3])
    entering = total + jnp.exp(log) * prior_ref[...]
    for k, out_ref in enumerate(refs[-4:]):
        decay = jnp.exp(before_ref[k, WIDTH : WIDTH + 1, :])
        out_ref[...] = (decay * entering + before_ref[k, 0:WIDTH, :]).astype(BF16)


def row_enter(place, parts, before, prior, after):
    pieces = pl.pallas_call(
        row_enter_kernel,
        out_shape=[jax.ShapeDtypeStruct((WIDTH, SLICE), BF16)] * 4,
        in_specs=[SMEM] + [VMEM] * 6 + [ANY] * len(after),
        out_specs=[VMEM] * 4,
        compiler_params=params(),
        cost_estimate=cost(16 * WIDTH * SLICE, 2**20),
        name="row_enter",
    )(place, *parts, before, prior, *after)
    return list(pieces)


def row_enter_all_kernel(place, p0, p1, p2, p3, before_ref, prior_ref, *refs):
    total, log = fold(place[3], (p0, p1, p2, p3), place[3])
    entering = total + jnp.exp(log) * prior_ref[...]
    for at in range(4):
        before = before_ref[lax.rem(at - place[2] + 4, 4)]
        decay = jnp.exp(before[WIDTH : WIDTH + 1, :])
        refs[-1][at] = (decay * entering + before[0:WIDTH, :]).astype(BF16)


def row_enter_all(place, parts, before, prior, after):
    return pl.pallas_call(
        row_enter_all_kernel,
        out_shape=jax.ShapeDtypeStruct((4, WIDTH, SLICE), BF16),
        in_specs=[SMEM] + [VMEM] * 6 + [ANY] * len(after),
        out_specs=VMEM,
        compiler_params=params(),
        cost_estimate=cost(16 * WIDTH * SLICE, 2**20),
        name="row_enter",
    )(place, *parts, before, prior, *after)


def enter_all_kernel(place, parts_ref, keep_ref, got_ref, *refs):
    mine_ref, other_ref, chip = refs[-3:]
    first = place[0] == 0
    for at in range(4):
        chip[:, at * SLICE : (at + 1) * SLICE] = parts_ref[at].astype(F32)
    entering = chip[...]
    state0 = jnp.where(first, keep_ref[...], got_ref[...])
    second = jnp.exp(state0[WIDTH : WIDTH + 1]) * entering + state0[0:WIDTH]
    mine_ref[...] = jnp.where(first, entering, second).astype(BF16)
    other_ref[...] = jnp.where(first, second, entering).astype(BF16)


def entering_state_all(place, parts, keep, got, after=()):
    shape = jax.ShapeDtypeStruct((WIDTH, SPLIT), BF16)
    return pl.pallas_call(
        enter_all_kernel,
        out_shape=(shape, shape),
        in_specs=[SMEM] + [VMEM] * 3 + [ANY] * len(after),
        out_specs=(VMEM, VMEM),
        scratch_shapes=[pltpu.VMEM((WIDTH, SPLIT), F32)],
        compiler_params=params(),
        cost_estimate=cost(8 * WIDTH * SPLIT, 2 * 2**20),
        name="entering_state",
    )(place, parts, keep, got, *after)


def enter_kernel(place, p0, p1, p2, p3, keep_ref, got_ref, *refs):
    mine_ref, other_ref, chip = refs[-3:]
    first = place[0] == 0
    for k, part in enumerate((p0, p1, p2, p3)):
        chip[:, slice_of(place, -k)] = part[...].astype(F32)
    entering = chip[...]
    state0 = jnp.where(first, keep_ref[...], got_ref[...])
    second = jnp.exp(state0[WIDTH : WIDTH + 1]) * entering + state0[0:WIDTH]
    mine_ref[...] = jnp.where(first, entering, second).astype(BF16)
    other_ref[...] = jnp.where(first, second, entering).astype(BF16)


def entering_state(place, parts, keep, got, after=()):
    shape = jax.ShapeDtypeStruct((WIDTH, SPLIT), BF16)
    return pl.pallas_call(
        enter_kernel,
        out_shape=(shape, shape),
        in_specs=[SMEM] + [VMEM] * 6 + [ANY] * len(after),
        out_specs=(VMEM, VMEM),
        scratch_shapes=[pltpu.VMEM((WIDTH, SPLIT), F32)],
        compiler_params=params(),
        cost_estimate=cost(8 * WIDTH * SPLIT, 2 * 2**20),
        name="entering_state",
    )(place, *parts, keep, got, *after)


def gated_kernel(place, mine_ref, other_ref, read_ref, plain_ref, scale_ref, gain_ref, *refs):
    top_ref, low_ref, stat_ref = refs[-3:]
    read = read_ref[...]
    width = 256
    part = None
    for start in range(0, LANES, width):
        at = slice(start, start + width)
        source = slice(start % SPLIT, start % SPLIT + width)
        mine = place[0] == start // SPLIT
        entering = jnp.where(mine, mine_ref[:, source], other_ref[:, source])
        carried = jnp.dot(read, entering, preferred_element_type=F32)
        gated = plain_ref[:, at] + scale_ref[:, at] * carried
        result = (gated * gain_ref[:, at]).astype(BF16)
        top_ref[:, at] = result[:HALF]
        low_ref[:, at] = result[HALF:]
        square = gated * gated
        square = square[:, :128] + square[:, 128:]
        part = square if part is None else part + square
    row = jnp.sum(part.T, axis=0, keepdims=True)
    stat_ref[...] = jnp.zeros_like(stat_ref)
    stat_ref[:, 0:ROWS] = stack_rows(three(row), 16).astype(BF16)


def gated_part(place, mine, other, reads, plain, scale, gain, after):
    return pl.pallas_call(
        gated_kernel,
        out_shape=(
            jax.ShapeDtypeStruct((HALF, LANES), BF16),
            jax.ShapeDtypeStruct((HALF, LANES), BF16),
            jax.ShapeDtypeStruct((16, PIECE), BF16),
        ),
        in_specs=[SMEM] + [VMEM] * 6 + [ANY] * len(after),
        out_specs=[VMEM] * 3,
        compiler_params=params(),
        cost_estimate=cost(2 * ROWS * WIDTH * LANES, 6 * 2**20),
        name="gated_part",
    )(place, mine, other, reads, plain, scale, gain, *after)


def multiply(lefts, weights, out):
    depth = LANES // len(weights)
    for row, ref in enumerate(lefts):
        rows = row * HALF
        total = None
        for part, weight in enumerate(weights):
            at = slice(part * depth, (part + 1) * depth)
            term = jnp.dot(ref[:, at], weight[...], preferred_element_type=F32)
            total = term if total is None else total + term
        out[rows : rows + HALF, :] = total.astype(BF16)


def hand_out(place, total, outs):
    core, x, z = place[0], place[1], place[3]
    for k in range(4):
        out_ref = outs[k if k < 3 or len(outs) == 4 else 4]
        j = lax.rem(x + k - z + 4, 4)
        for half in range(2):
            at = slice(half * 256, (half + 1) * 256)
            side = lax.rem(half + core, 2)
            if len(outs) == 5 and k == 2:
                outs[2 + half][...] = total[j, side]
            else:
                out_ref[0 : total.shape[2], at] = total[j, side]


def project_kernel(tall, count, far, stats, ring, place, *refs):
    lefts, refs = refs[:tall], refs[tall:]
    outs, total = refs[-5 - ring : -1], refs[-1]
    for side in range(2):
        own, above, below = refs[side * count : side * count + 3]
        beyond = refs[side * count + 3 : side * count + 3 + far]
        for j, parts in enumerate(((own,), (above,), beyond, (below,))):
            multiply(lefts, parts, total.at[j, side])
    hand_out(place, total, outs)
    for stat in stats:
        for out_ref in outs:
            out_ref[tall * HALF :, :] = refs[stat][...]


def project(place, lefts, weights, stats=None, after=(), ring=False):
    tall = len(lefts)
    rows = tall * HALF + (0 if stats is None else 16)
    extra = () if stats is None else (stats,)
    widths = [PIECE, PIECE, 256, 256, PIECE] if ring else [PIECE] * 4
    count = len(weights) // 2
    place_of_stats = (len(weights),) * len(extra)
    pieces = pl.pallas_call(
        functools.partial(project_kernel, tall, count, count - 3, place_of_stats, int(ring)),
        in_specs=[SMEM] + [VMEM] * (tall + len(weights) + len(extra)) + [ANY] * len(after),
        out_specs=[VMEM] * len(widths),
        out_shape=[jax.ShapeDtypeStruct((rows, width), BF16) for width in widths],
        scratch_shapes=[pltpu.VMEM((4, 2, tall * HALF, 256), BF16)],
        compiler_params=params(24),
        cost_estimate=cost(2 * ROWS * LANES * 4 * PIECE, 10 * 2**20),
        name="project",
    )(place, *lefts, *weights, *extra, *after)
    return list(pieces)


def hold_kernel(value_ref, out_ref):
    out_ref[...] = value_ref[...]


def hold(value, micros):
    return pl.pallas_call(
        hold_kernel,
        out_shape=jax.ShapeDtypeStruct(value.shape, value.dtype),
        in_specs=[VMEM],
        out_specs=VMEM,
        compiler_params=params(),
        cost_estimate=pl.CostEstimate(
            flops=micros * 10**9, bytes_accessed=2**20, transcendentals=0
        ),
        name="hold",
    )(value)


def near_kernel(top_ref, low_ref, *refs):
    out = refs[-1]
    for side in range(2):
        own, above, below = refs[3 * side : 3 * side + 3]
        for j, part in ((0, own), (1, above), (2, below)):
            multiply((top_ref, low_ref), (part,), out.at[j, side])


def project_near(top, low, weights, after):
    return pl.pallas_call(
        near_kernel,
        in_specs=[VMEM] * 8 + [ANY] * len(after),
        out_specs=VMEM,
        out_shape=jax.ShapeDtypeStruct((3, 2, ROWS, 256), BF16),
        compiler_params=params(24),
        cost_estimate=cost(2 * ROWS * LANES * 3 * PIECE, 2 * 4 * 2**20),
        name="project_near",
    )(top, low, *weights, *after)


def far_kernel(place, top_ref, low_ref, *refs):
    near, stat_ref, outs, total = refs[-7], refs[-6], refs[-5:-1], refs[-1]
    for j, source in ((0, 0), (1, 1), (3, 2)):
        total[j] = near[source]
    parts = (len(refs) - 7) // 2
    for side in range(2):
        multiply((top_ref, low_ref), refs[parts * side : parts * side + parts], total.at[2, side])
    hand_out(place, total, outs)
    for out_ref in outs:
        out_ref[ROWS:, :] = stat_ref[...]


def project_far(place, top, low, weights, near, stats):
    pieces = pl.pallas_call(
        far_kernel,
        in_specs=[SMEM] + [VMEM] * (4 + len(weights)),
        out_specs=[VMEM] * 4,
        out_shape=[jax.ShapeDtypeStruct((ROWS + 16, PIECE), BF16)] * 4,
        scratch_shapes=[pltpu.VMEM((4, 2, ROWS, 256), BF16)],
        compiler_params=params(24),
        cost_estimate=cost(2 * ROWS * LANES * PIECE, 2 * 2 * 2**20),
        name="project_far",
    )(place, top, low, *weights, near, stats)
    return list(pieces)


def add(parts, rows):
    total = parts[0][rows, :].astype(F32)
    for part in parts[1:]:
        total = total + part[rows, :].astype(F32)
    return total


def start_of(part):
    return ROWS if part.shape[0] > 2 * ROWS else 0


def sums_kernel(count, *refs):
    first, second, (down_ref, up_ref) = refs[:count], refs[count:-2], refs[-2:]
    for at, parts in ((0, first), (HALF, second)):
        row = start_of(parts[0])
        down_ref[at : at + HALF, :] = add(parts, slice(row, row + HALF)).astype(BF16)
        up_ref[at : at + HALF, :] = add(parts, slice(row + HALF, row + ROWS)).astype(BF16)


def neighbour_sums(first, second):
    shape = jax.ShapeDtypeStruct((ROWS, PIECE), BF16)
    return pl.pallas_call(
        functools.partial(sums_kernel, len(first)),
        out_shape=(shape, shape),
        in_specs=[VMEM] * (len(first) + len(second)),
        out_specs=(VMEM, VMEM),
        compiler_params=params(),
        cost_estimate=cost(8 * ROWS * PIECE, 10 * ROWS * PIECE * 2),
        name="neighbour_sums",
    )(*first, *second)


def sum_kernel(*refs):
    row = start_of(refs[0])
    refs[-1][...] = add(refs[:-1], slice(row, row + ROWS)).astype(BF16)


def far_sums(parts):
    return pl.pallas_call(
        sum_kernel,
        out_shape=jax.ShapeDtypeStruct((ROWS, PIECE), BF16),
        in_specs=[VMEM] * len(parts),
        out_specs=VMEM,
        compiler_params=params(),
        cost_estimate=cost(4 * ROWS * PIECE, 5 * ROWS * PIECE * 2),
        name="far_sums",
    )(*parts)


def merge_kernel(up_ref, down_ref, left_ref, right_ref, sum_up_ref, sum_down_ref):
    for ref, half_ref, out_ref, at in (
        (up_ref, left_ref, sum_up_ref, 0),
        (down_ref, right_ref, sum_down_ref, 256),
    ):
        out_ref[:, 256 - at : 512 - at] = ref[:, 256 - at : 512 - at]
        total = ref[:, at : at + 256].astype(F32) + half_ref[...].astype(F32)
        out_ref[:, at : at + 256] = total.astype(BF16)


def merge(up, down, left, right):
    shape = jax.ShapeDtypeStruct((ROWS, PIECE), BF16)
    return pl.pallas_call(
        merge_kernel,
        out_shape=(shape, shape),
        in_specs=[VMEM] * 4,
        out_specs=(VMEM, VMEM),
        compiler_params=params(),
        cost_estimate=cost(ROWS * PIECE, 5 * ROWS * PIECE * 2),
        name="merge",
    )(up, down, left, right)


def write_columns(out_ref, residual_ref, scale, total):
    for at in range(0, PIECE, 128):
        cols = slice(at, at + 128)
        out_ref[:, cols] = (residual_ref[:, cols].astype(F32) + scale * total[:, cols]).astype(BF16)


def finish_kernel(tall, place, p0, p1, p2, p3, up_ref, down_ref, residual_ref, _, out_ref, scale_ref):
    own = (p0, p1, p2, p3)
    step = pl.program_id(0)

    @pl.when(step == 0)
    def _():
        square = sum(unpack_rows(part[tall : tall + 16, 0:ROWS]) for part in own)
        row = lax.rsqrt(square / INNER + EPSILON)
        scale_ref[...] = jnp.broadcast_to(row, (128, ROWS)).T
        write_columns(out_ref, residual_ref, scale_ref[...], add(own, slice(0, ROWS)))

    for k, ref in ((1, up_ref), (2, down_ref)):

        @pl.when(step == k)
        def _(ref=ref):
            write_columns(out_ref, residual_ref, scale_ref[...], ref[...].astype(F32))


OUT = jax.ShapeDtypeStruct((ROWS, 4 * PIECE), BF16)


def finish(place, own, up, down, residual, after):
    block = pl.BlockSpec(
        (ROWS, PIECE), lambda i, place: (0, lax.rem(place[2] + jnp.where(i == 2, 3, i), 4))
    )
    return pl.pallas_call(
        functools.partial(finish_kernel, own[0].shape[0] - 16),
        grid_spec=pltpu.PrefetchScalarGridSpec(
            num_scalar_prefetch=1,
            grid=(3,),
            in_specs=[whole(own[0].shape)] * 4 + [whole((ROWS, PIECE))] * 2 + [block, ANY],
            out_specs=[block, whole((ROWS, 128))],
        ),
        out_shape=(OUT, jax.ShapeDtypeStruct((ROWS, 128), F32)),
        compiler_params=params(),
        cost_estimate=cost(4 * ROWS * 3 * PIECE, 3 * 2**20),
        name="finish",
    )(place, *own, up, down, residual, after)


def finish_far_kernel(place, far_ref, scale_ref, residual_ref, _, out_ref):
    write_columns(out_ref, residual_ref, scale_ref[...], far_ref[...].astype(F32))


def finish_far(place, far, scale, residual, out):
    block = pl.BlockSpec((ROWS, PIECE), lambda i, place: (0, lax.rem(place[2] + 2, 4)))
    return pl.pallas_call(
        finish_far_kernel,
        grid_spec=pltpu.PrefetchScalarGridSpec(
            num_scalar_prefetch=1,
            grid=(1,),
            in_specs=[whole((ROWS, PIECE)), whole((ROWS, 128)), block, ANY],
            out_specs=block,
        ),
        out_shape=OUT,
        input_output_aliases={4: 0},
        compiler_params=params(),
        cost_estimate=cost(4 * ROWS * PIECE, 2**20),
        name="finish_far",
    )(place, far, scale, residual, out)


def shift(value, axis, by):
    return lax.ppermute(value, axis, [(i, (i + by) % 4) for i in range(4)])


def swap(value):
    return lax.ppermute(value, "core", [(0, 1), (1, 0)])


def later(values, events):
    return lax.optimization_barrier((tuple(values), tuple(events)))[0]


def scatter(pieces, axis="x"):
    if len(pieces) == 4:
        return [pieces[0]] + [shift(pieces[k], axis, k) for k in (1, 2, 3)]
    here, up, left, right, down = pieces
    up, down = merge(up, down, shift(left, axis, 1), shift(right, axis, -1))
    return [here, shift(up, axis, 1), shift(down, axis, -1)]


def body(
    head_values,
    gate_values,
    write_keys,
    read_keys,
    step_size,
    decay_rate,
    skip_weight,
    prior_state,
    norm_gain,
    out_weight,
    residual,
):
    place = jnp.stack([lax.axis_index(name) for name in ("core", "x", "y", "z")]).astype(jnp.int32)

    steps = step_size.T
    packed = jnp.concatenate([steps, -steps * decay_rate[:, None]], axis=0)
    from_below, from_above = shift(out_weight, "z", 1), shift(out_weight, "z", -1)
    keep, send = local_state(place, head_values, write_keys, packed)
    got = swap(send)
    weight = [out_weight, from_above, from_below]
    swapped = [swap(out_weight)]
    chips = chip_total(place, keep, got, [])
    sources = (head_values, gate_values, write_keys, read_keys, packed, skip_weight[None, :])
    plain, scale = plain_part(*sources, chips[0])
    prior = turned_prior(place, prior_state, chips[0])
    row, before = row_total(place, scatter(chips, "y"), (prior, plain,))
    rows = scatter([row] * 4, "z")
    swapped += [swap(part) for part in later(weight[1:], rows[1:])]
    entered = row_enter(place, rows, before, prior, [*weight[1:]])
    depth = out_weight.shape[0] // 2
    halves = (from_below[:depth], from_above[depth:])
    halves = later(halves, entered)
    entering = scatter(entered, "y")
    far_weight = [shift(halves[0], "z", 1), shift(halves[1], "z", -1)]
    mine, other = entering_state(place, entering, keep, got, [*swapped])
    other = swap(other)
    gain = norm_gain[None, :]
    top, low, stats = gated_part(place, mine, other, read_keys, plain, scale, gain, [])
    top_go = top
    top_below, top_above = shift(top_go, "y", 1), shift(top_go, "y", -1)
    near = project_near(top, low, weight + swapped, [])
    far_swapped = [swap(part) for part in later(far_weight, [near])]
    weights = weight + far_weight + swapped + far_swapped
    own = project_far(place, top, low, far_weight + far_swapped, near, stats)
    low_go = low
    (low_go,) = later([low], [top_below, top_above])
    low_below, low_above = shift(low_go, "y", 1), shift(low_go, "y", -1)
    own = scatter(own)
    first = project(place, [top_below, top_above], weights, None, [], False)
    go = (top_below, low_above)
    go = later(go, (top_above, low_below, first[0]))
    top_far, low_far = shift(go[0], "y", 1), shift(go[1], "y", -1)
    first = scatter(first)
    second = project(place, [low_below, low_above], weights, None, own[1:] + first[:1], False)
    second = scatter(second)
    far = project(place, [top_far, low_far], weights, None, second[:1], False)
    far = scatter(far)

    down, up = neighbour_sums(first, second)
    from_above = shift(down, "y", -1)
    from_below = shift(up, "y", 1)
    far = far_sums(far)
    from_far = shift(far, "y", 2)
    out, scale = finish(place, own, from_above, from_below, residual, far)
    return finish_far(place, from_far, scale, residual, out)


def solution(mesh):
    grid = Mesh(mesh.devices.reshape(4, 4, 2, 4), ("z", "y", "core", "x"))
    ctx = ("z", "y", "core")
    in_specs = (
        P(ctx, "x"),
        P(ctx, "x"),
        P(ctx, None),
        P(ctx, None),
        P(ctx, "x"),
        P("x"),
        P("x"),
        P("x", None, None),
        P("x"),
        P("x", ctx),
        P(ctx, "x"),
    )
    return jax.shard_map(
        body, mesh=grid, in_specs=in_specs, out_specs=P(ctx, "x"), check_vma=False
    )
```
